512 devices in a mesh: row: 8 (over y), col: 32 (over z, x), cores: 2 (over core).
Axes of the slice: x: 4, y: 8, z: 8, core: 2. Of those that a mesh axis runs over, the one named last changes fastest.
Arguments:
- root_rhs: bfloat16 [20480, 256], P(('col', 'cores')), may hold values from -6 to 6
- root_inverse: bfloat16 [20480, 20480], P(('col', 'cores'), 'row'), as said below
- child_rhs: bfloat16 [2, 10240, 256], P('cores', 'col'), may hold values from -6 to 6
- child_inverse: bfloat16 [2, 10240, 10240], P('cores', 'col', 'row'), as said below
- coupling: bfloat16 [2, 20480, 10240], P('cores', 'row', 'col'), may hold values from -0.0390625 to 0.0390625
- block_map: int32 [2, 160], replicated, may hold values from 0 to 159, as said below
- block_count: int32 [2], replicated, may hold values from 80 to 160, as said below
Outputs:
- root_solution: bfloat16 [20480, 256], P(('row', 'col', 'cores'))
- child_solution: bfloat16 [2, 10240, 256], P('cores', ('row', 'col'))
The draws below stay inside these ranges and needn't reach their ends.
Inputs may be any that keep to these rules, and one draw needn't show every extreme that they name: `root_inverse`: entries whose row index is below the column index are zero. `child_inverse`: entries whose row index is below the column index are zero. `block_map`: the slots of a child form aligned groups of 20; range p holds blocks p * 20 to p * 20 + 19. In each group at most 3 slots name blocks of one range, some range is named exactly 3 times, and slots of one group naming one range name different blocks. Slots k of child f with k >= block_count[f] are padding. Some child has 160 live slots.
All inputs are finite; a program needn't handle non-finite values.
Results may differ from the reference program's by a relative error of at most 0.0054.
Values may be sent and summed in bfloat16 or wider, within the bound.
A program may use at most 64 MiB of HBM per device.

```python
import math
import jax
import jax.numpy as jnp
from jax import lax

BLOCK = 128
CASES = 256
ROOT_SEP = 20480
CHILD_SEP = 10240
FRONTS = 2
ROOT_BLOCKS = 160
SLOTS = 160
GROUP = 20
RANGE = 20
CAPACITY = 3
N_ROW = 8


def triangle(noise, diagonal, order):
    rows_index = jnp.arange(order, dtype=jnp.int32)[:, None]
    cols_index = jnp.arange(order, dtype=jnp.int32)[None, :]
    lower_part = jnp.where(rows_index > cols_index, noise, 0.0)
    return lower_part + jnp.where(rows_index == cols_index, diagonal[..., None, :], 0.0)


def draw_root_inverse(key, part):
    key = jax.random.fold_in(key, 21)
    key_noise, key_diag = jax.random.split(key)
    noise = jax.random.normal(key_noise, (ROOT_SEP, ROOT_SEP), jnp.float32)
    diagonal = jax.random.uniform(key_diag, (ROOT_SEP,), jnp.float32, 0.6, 1.4)
    return triangle(noise * (0.8 / math.sqrt(ROOT_SEP)), diagonal, ROOT_SEP).astype(jnp.bfloat16)


def draw_child_inverse(key, part):
    key = jax.random.fold_in(key, 22)
    key_noise, key_diag = jax.random.split(key)
    noise = jax.random.normal(key_noise, (FRONTS, CHILD_SEP, CHILD_SEP), jnp.float32)
    diagonal = jax.random.uniform(key_diag, (FRONTS, CHILD_SEP), jnp.float32, 0.6, 1.4)
    return triangle(noise * (0.8 / math.sqrt(CHILD_SEP)), diagonal, CHILD_SEP).astype(jnp.bfloat16)


def one_group(key):
    key_favored, key_shuffle, key_place, key_within = jax.random.split(key, 4)
    pool_size = N_ROW * CAPACITY
    owner_pool = jnp.arange(pool_size, dtype=jnp.int32) // CAPACITY
    favored = jax.random.randint(key_favored, (), 0, N_ROW, dtype=jnp.int32)
    shuffle = jax.random.permutation(key_shuffle, jnp.arange(pool_size, dtype=jnp.int32))
    priority = shuffle + jnp.where(owner_pool == favored, -pool_size, 0).astype(jnp.int32)
    ordering = jnp.argsort(priority, stable=True)
    owners = owner_pool[ordering[:GROUP]]
    owners = owners[jax.random.permutation(key_place, jnp.arange(GROUP, dtype=jnp.int32))]
    positions = jnp.arange(GROUP, dtype=jnp.int32)
    same_owner = owners[:, None] == owners[None, :]
    earlier = positions[None, :] < positions[:, None]
    owner_rank = jnp.sum(same_owner & earlier, axis=1).astype(jnp.int32)
    within_keys = jax.random.split(key_within, N_ROW)
    within = jax.vmap(jax.random.permutation, in_axes=(0, None))(within_keys, jnp.arange(RANGE, dtype=jnp.int32))
    return (owners * RANGE + within[owners, owner_rank]).astype(jnp.int32)


def draw_block_map(key, part):
    key = jax.random.fold_in(key, 11)
    group_keys = jax.random.split(key, FRONTS * N_ROW)
    grouped = jax.vmap(one_group)(group_keys)
    return grouped.reshape(FRONTS, SLOTS)


def draw_block_count(key, part):
    key = jax.random.fold_in(key, 12)
    key_count, key_full = jax.random.split(key)
    counts = jax.random.randint(key_count, (FRONTS,), SLOTS // 2, SLOTS + 1, dtype=jnp.int32)
    fullest = jax.random.randint(key_full, (), 0, FRONTS, dtype=jnp.int32)
    return jnp.where(jnp.arange(FRONTS, dtype=jnp.int32) == fullest, SLOTS, counts).astype(jnp.int32)


def block_scale(rng, extent, cuts, low, top_value):
    level, own = 1.0, jax.random.fold_in(rng, 6)
    for dim, blocks in cuts:
        heights = jnp.exp(jax.random.uniform(jax.random.fold_in(own, dim), (blocks,), jnp.float32, low / len(cuts), top_value / len(cuts)))
        level = level * jnp.repeat(heights, extent[dim] // blocks).reshape([-1 if axis == dim else 1 for axis in range(len(extent))])
    return level


def centred(key, extent, deviation, bound, cuts=(), kind=jnp.bfloat16):
    factor_of = block_scale(key, extent, cuts, -0.22, 0.18) if cuts else 1.0
    entries = jax.random.normal(key, extent, jnp.float32) * deviation * factor_of
    return jnp.minimum(jnp.maximum(entries, -bound), bound).astype(kind)


def setup_inputs(seed: int = 0) -> dict:
    streams_of = jax.random.split(jax.random.key(seed), 8)
    return {
        "root_rhs": centred(streams_of[0], (ROOT_SEP, CASES), 1.0, 6.0, ((0, 64),)),
        "root_inverse": draw_root_inverse(jax.random.fold_in(streams_of[7], 71), 0),
        "child_rhs": centred(streams_of[2], (FRONTS, CHILD_SEP, CASES), 1.0, 6.0, ((0, 2), (1, 32))),
        "child_inverse": draw_child_inverse(jax.random.fold_in(streams_of[7], 71), 0),
        "coupling": centred(streams_of[4], (FRONTS, SLOTS * BLOCK, CHILD_SEP), (SLOTS * BLOCK) ** -0.5, 0.0390625, ((0, 2), (1, 8), (2, 32))),
        "block_map": draw_block_map(jax.random.fold_in(streams_of[7], 71), 0),
        "block_count": draw_block_count(jax.random.fold_in(streams_of[7], 71), 0),
    }


def contract_rows(matrix, right):
    return lax.dot_general(matrix, right, (((0,), (0,)), ((), ())), preferred_element_type=jnp.float32)


def reference(root_rhs, root_inverse, child_rhs, child_inverse, coupling, block_map, block_count):
    root_solution = contract_rows(root_inverse, root_rhs).astype(jnp.bfloat16)
    all_blocks = root_solution.reshape(ROOT_BLOCKS, BLOCK, CASES)
    slot_ids = jnp.arange(SLOTS, dtype=jnp.int32)
    solutions = []
    for front_index in range(FRONTS):
        picked = jnp.take(all_blocks, block_map[front_index], axis=0)
        alive_slots = slot_ids < block_count[front_index]
        picked = jnp.where(alive_slots[:, None, None], picked, jnp.zeros((), jnp.bfloat16))
        picked = picked.reshape(SLOTS * BLOCK, CASES)
        coupled = contract_rows(coupling[front_index], picked)
        reduced = (child_rhs[front_index].astype(jnp.float32) - coupled).astype(jnp.bfloat16)
        solutions.append(contract_rows(child_inverse[front_index], reduced).astype(jnp.bfloat16))
    return root_solution, jnp.stack(solutions)
```

```python
import functools

import jax
import jax.numpy as jnp
from jax import lax
from jax.experimental import pallas as pl
from jax.experimental.pallas import tpu as pltpu
from jax.sharding import PartitionSpec as P

BLOCK = 128
CAP = 3
GRID = {32: (4, 8), 4: (2, 2)}
MESH = pl.DeviceIdType.MESH
BF = jnp.bfloat16
F32 = jnp.float32


class Sizes:
    def __init__(self, mesh, root_rhs, root_inverse, child_inverse, coupling, block_map):
        self.NY = mesh.shape["row"]
        self.NX, self.NZ = GRID[mesh.shape["col"]]
        self.Q = self.NX * self.NZ
        self.S1, self.C = root_rhs.shape
        self.T1 = root_inverse.shape[1]
        self.NB = self.T1 // BLOCK
        self.HB = self.NB // 2
        self.CB = 2
        self.NCH = self.HB // self.CB
        self.S3, self.T3 = child_inverse.shape[1:]
        self.U = coupling.shape[1]
        self.G = self.U // BLOCK
        self.CY = self.C // self.NY
        self.TO = self.T1 // (2 * self.Q)
        self.TC = self.T3 // self.Q
        self.TZ = self.T1 // self.NZ
        starts = [self.TZ * z // BLOCK for z in range(self.NZ)]
        ends = [-(-self.TZ * (z + 1) // BLOCK) for z in range(self.NZ)]
        self.SPAN = max(e - s for s, e in zip(starts, ends))


def far_first(n):
    return sorted(range(1, n), key=lambda d: (-min(d, n - d), d))


def kernel(
    sz, rrhs, rinv, crhs, cinv, coup, bmap, bcnt, rout, cout, *,
    rinv_v, coup_v, cinv_v, cit, rhs_t, crhs_t, cs, cr, own, xs, xr, zacc, zs, zr, sol,
    ysd, yrc, gath, lhs, ycs, y1s, ycr, red, o1, o2, ot, p5f, p5s, p5r, z5s, z5r, sel, pos,
    lsem, csem, xsem, zsem, c2sem, ysem, o1sem, o2sem, agx, agu, agd, y1sem, y2sem, p5sem, z5sem,
):
    NX, NZ, NY, NCH, CB, HB, NB, G = sz.NX, sz.NZ, sz.NY, sz.NCH, sz.CB, sz.HB, sz.NB, sz.G
    r, c, k = lax.axis_index("row"), lax.axis_index("col"), lax.axis_index("cores")
    z, x = c // NX, lax.rem(c, NX)

    def xd(d):
        return lax.rem(x + d + NX, NX)

    def zd(d):
        return lax.rem(z + d + NZ, NZ)

    def yd(d):
        return lax.rem(r + d + NY, NY)

    def dev_x(d):
        return (r, z * NX + xd(d), k)

    def dev_z(d):
        return (r, zd(d) * NX + x, k)

    def dev_y(d):
        return (yd(d), c, k)

    dev_c = (r, c, 1 - k)
    sent = []

    def send(src, dst, sem, idx, dev):
        cp = pltpu.make_async_remote_copy(
            src_ref=src, dst_ref=dst, send_sem=sem.at[(0,) + idx], recv_sem=sem.at[(1,) + idx],
            device_id=dev, device_id_type=MESH,
        )
        cp.start()
        sent.append(cp)

    def arrived(ref, sem, idx):
        pltpu.make_async_remote_copy(
            src_ref=ref, dst_ref=ref, send_sem=sem.at[(0,) + idx], recv_sem=sem.at[(1,) + idx],
            device_id=dev_c, device_id_type=MESH,
        ).wait_recv()

    barrier = pltpu.get_barrier_semaphore()
    peers = (
        [dev_c]
        + [dev_x(d) for d in range(1, NX)]
        + [dev_z(d) for d in range(1, NZ)]
        + [dev_y(d) for d in range(1, NY)]
    )
    for dev in peers:
        pl.semaphore_signal(barrier, inc=1, device_id=dev, device_id_type=MESH)

    half = HB * BLOCK
    loads = [
        pltpu.make_async_copy(
            rinv.at[:, pl.ds(pl.multiple_of((1 - k) * half, BLOCK), half)],
            rinv_v.at[:, pl.ds(pl.multiple_of((1 - k) * half, BLOCK), half)], lsem.at[0]),
        pltpu.make_async_copy(
            rinv.at[:, pl.ds(pl.multiple_of(k * half, BLOCK), half)],
            rinv_v.at[:, pl.ds(pl.multiple_of(k * half, BLOCK), half)], lsem.at[1]),
        pltpu.make_async_copy(cinv.at[0], cinv_v, lsem.at[2]),
        pltpu.make_async_copy(coup.at[0], coup_v, lsem.at[3]),
    ]
    for cp in loads:
        cp.start()
    rhs_t[...] = rrhs[...].astype(F32).T.astype(BF)

    def partial(which, dst, ch):
        off = pl.multiple_of(which * half + ch * CB * BLOCK, BLOCK)
        v = jnp.dot(rhs_t[...], rinv_v[:, pl.ds(off, CB * BLOCK)], preferred_element_type=F32)
        for b in range(CB):
            dst[ch, :, b] = v[:, b * BLOCK:(b + 1) * BLOCK].reshape(sz.Q, 8, BLOCK)

    loads[0].wait()
    for ch in range(NCH):
        partial(1 - k, cs, ch)
        if ch == 0:
            pl.semaphore_wait(barrier, len(peers))
        send(cs.at[ch], cr.at[ch], csem, (ch,), dev_c)
    loads[1].wait()
    for ch in range(NCH):
        partial(k, own, ch)

    mine_x = pl.ds(x * NZ, NZ)
    for ch in range(NCH):
        arrived(cr.at[ch], csem, (ch,))
        for d in range(1, NX):
            rows = pl.ds(xd(d) * NZ, NZ)
            xs[ch, d] = (own[ch, rows] + cr[ch, rows]).astype(BF)
            send(xs.at[ch, d], xr.at[ch, d], xsem, (ch, d), dev_x(d))

    def choose(t, _):
        cnt = jnp.int32(0)
        got = [jnp.int32(0)] * CAP
        for s in range(G):
            b = bmap[k, t * G + s] - r * NB
            inside = jnp.logical_and(b >= 0, b < NB)
            for j in range(CAP):
                got[j] = jnp.where(jnp.logical_and(inside, cnt == j), b, got[j])
            cnt = cnt + jnp.where(inside, 1, 0)
        for j in range(CAP):
            sel[t * CAP + j] = got[j]
        return 0

    lax.fori_loop(0, NY, choose, 0)
    ranges = [lax.div(bmap[k, r * G + s], jnp.int32(NB)) for s in range(G)]
    for s in range(G):
        rank = jnp.int32(0)
        for e in range(s):
            rank = rank + jnp.where(ranges[e] == ranges[s], 1, 0)
        pos[s] = ranges[s] * CAP + jnp.minimum(rank, CAP - 1)

    for ch in range(NCH):
        acc = own[ch, mine_x] + cr[ch, mine_x]
        for d in range(1, NX):
            arrived(xr.at[ch, d], xsem, (ch, d))
            acc = acc + xr[ch, d].astype(F32)
        zacc[ch] = acc
        zs[ch] = acc.astype(BF)
        for d in far_first(NZ):
            send(zs.at[ch, zd(d)], zr.at[ch, d], zsem, (ch, d), dev_z(d))

    loads[2].wait()
    for j in range(sz.T3 // BLOCK):
        cols = slice(j * BLOCK, (j + 1) * BLOCK)
        cit[cols, :] = cinv_v[:, cols].astype(F32).T.astype(BF)
    crhs_t[...] = crhs[0].astype(F32).T

    for ch in range(NCH):
        acc = zacc[ch, z]
        for d in range(1, NZ):
            arrived(zr.at[ch, d], zsem, (ch, d))
            acc = acc + zr[ch, d].astype(F32)
        sol[pl.ds(k * HB + ch * CB, CB)] = acc.astype(BF)
    mine = pl.ds(k * HB, HB)
    send(sol.at[mine], sol.at[mine], c2sem, (0,), dev_c)
    arrived(sol.at[pl.ds((1 - k) * HB, HB)], c2sem, (0,))

    for d in far_first(NY) + [0]:
        t = yd(d)
        for j in range(CAP):
            v = sol[sel[t * CAP + j]]
            if d:
                ysd[d, j] = v
            else:
                yrc[r, j] = v
        if d:
            send(ysd.at[d], yrc.at[r], ysem, (d,), dev_y(d))
    def first_block(zz):
        return (sz.TZ * zz) // BLOCK

    for d in far_first(NZ):
        send(sol.at[pl.ds(first_block(zd(d)), sz.SPAN)], o1.at[z], o1sem, (d,), dev_z(d))
    o1[z] = sol[pl.ds(first_block(z), sz.SPAN)]

    q = x * NZ + z
    for d in range(1, NY):
        arrived(yrc.at[yd(-d)], ysem, (d,))
    for s in range(G):
        p = pos[s]
        v = yrc[lax.div(p, jnp.int32(CAP)), lax.rem(p, jnp.int32(CAP))]
        alive = r * G + s < bcnt[k]
        gath[q, s] = jnp.where(alive, v.astype(F32), 0.0).astype(BF)

    up, down = dev_z(1), dev_z(-1)
    mid = NZ // 2

    def forward(e, h, piece):
        if h < mid or (h == mid and e < NX // 2):
            send(gath.at[piece], gath.at[piece], agu, (e, h), up)
        if h < mid or (h == mid and e >= NX // 2):
            send(gath.at[piece], gath.at[piece], agd, (e, h), down)

    forward(0, 1, q)
    for d in range(1, NX):
        send(gath.at[q], gath.at[q], agx, (d,), dev_x(d))
    for e in range(1, NX):
        piece = xd(-e) * NZ + z
        arrived(gath.at[piece], agx, (e,))
        forward(e, 1, piece)
    for h in range(1, mid + 1):
        for e in range(NX):
            if h < mid or (h == mid and e < NX // 2):
                piece = xd(-e) * NZ + zd(-h)
                arrived(gath.at[piece], agu, (e, h))
                if h + 1 < mid or (h + 1 == mid and e < NX // 2):
                    send(gath.at[piece], gath.at[piece], agu, (e, h + 1), up)
            if h < mid or (h == mid and e >= NX // 2):
                piece = xd(-e) * NZ + zd(h)
                arrived(gath.at[piece], agd, (e, h))
                if h + 1 < mid or (h + 1 == mid and e >= NX // 2):
                    send(gath.at[piece], gath.at[piece], agd, (e, h + 1), down)

    loads[3].wait()
    for s in range(G):
        lhs[:, s * BLOCK:(s + 1) * BLOCK] = gath[:, s].reshape(sz.C, BLOCK)
    prod = jnp.dot(lhs[...], coup_v[...], preferred_element_type=F32)
    ycs[...] = prod.reshape(NY, sz.CY, sz.S3)
    for d in far_first(NY):
        y1s[d] = ycs[yd(d)].astype(BF)
        send(y1s.at[d], ycr.at[d], y1sem, (d,), dev_y(d))

    for d in range(1, NZ):
        arrived(o1.at[zd(-d)], o1sem, (d,))
    for d in range(1, NX):
        send(o1, o2.at[x], o2sem, (d,), dev_x(d))
    o2[x] = o1[...]

    acc = ycs[r]
    for d in range(1, NY):
        arrived(ycr.at[d], y1sem, (d,))
        acc = acc + ycr[d].astype(F32)
    mine_y = pl.ds(pl.multiple_of(r * sz.CY, sz.CY), sz.CY)
    red[r] = (crhs_t[mine_y, :] - acc).astype(BF)
    for d in far_first(NY):
        send(red.at[r], red.at[r], y2sem, (d,), dev_y(d))

    for d in range(1, NX):
        arrived(o2.at[xd(-d)], o2sem, (d,))
    for b in range(sz.SPAN):
        ot[b * BLOCK:(b + 1) * BLOCK, :] = o2[:, :, b].astype(F32).reshape(sz.C, BLOCK).T
    first_row = sz.TZ * z + (2 * x + k) * sz.TO - first_block(z) * BLOCK
    rout[...] = ot[pl.ds(pl.multiple_of(first_row, 8), sz.TO), :].astype(BF)

    for d in range(1, NY):
        arrived(red.at[yd(-d)], y2sem, (d,))
    reduced = red[...].reshape(sz.C, sz.S3)
    rows_z = NX * sz.TC
    for d in far_first(NZ) + [0]:
        rows = pl.ds(pl.multiple_of(zd(d) * rows_z, rows_z), rows_z)
        v = lax.dot_general(cit[rows, :], reduced, (((1,), (1,)), ((), ())), preferred_element_type=F32)
        p5f[d] = v.reshape(NX, sz.TC, sz.C)
        for e in range(1, NX):
            p5s[d, e] = p5f[d, xd(e)].astype(BF)
            send(p5s.at[d, e], p5r.at[d, e], p5sem, (d, e), dev_x(e))
    for d in far_first(NZ) + [0]:
        acc = p5f[d, x]
        for e in range(1, NX):
            arrived(p5r.at[d, e], p5sem, (d, e))
            acc = acc + p5r[d, e].astype(F32)
        if d:
            z5s[d] = acc.astype(BF)
            send(z5s.at[d], z5r.at[d], z5sem, (d,), dev_z(d))
    for d in far_first(NZ):
        arrived(z5r.at[d], z5sem, (d,))
        acc = acc + z5r[d].astype(F32)
    cout[0] = acc.astype(BF)

    for cp in sent:
        cp.wait_send()


def per_device(mesh, root_rhs, root_inverse, child_rhs, child_inverse, coupling, block_map, block_count):
    sz = Sizes(mesh, root_rhs, root_inverse, child_inverse, coupling, block_map)
    NX, NZ, NY, NCH, CB, Q, G = sz.NX, sz.NZ, sz.NY, sz.NCH, sz.CB, sz.Q, sz.G
    vmem = pl.BlockSpec(memory_space=pltpu.VMEM)
    smem = pl.BlockSpec(memory_space=pltpu.SMEM)
    hbm = pl.BlockSpec(memory_space=pl.ANY)

    def dma(*shape):
        return pltpu.SemaphoreType.DMA((2,) + shape)

    scratch = dict(
        rinv_v=pltpu.VMEM((sz.S1, sz.T1), BF),
        coup_v=pltpu.VMEM((sz.U, sz.S3), BF),
        cinv_v=pltpu.VMEM((sz.S3, sz.T3), BF),
        cit=pltpu.VMEM((sz.T3, sz.S3), BF),
        rhs_t=pltpu.VMEM((sz.C, sz.S1), BF),
        crhs_t=pltpu.VMEM((sz.C, sz.S3), F32),
        cs=pltpu.VMEM((NCH, Q, CB, 8, BLOCK), F32),
        cr=pltpu.VMEM((NCH, Q, CB, 8, BLOCK), F32),
        own=pltpu.VMEM((NCH, Q, CB, 8, BLOCK), F32),
        xs=pltpu.VMEM((NCH, NX, NZ, CB, 8, BLOCK), BF),
        xr=pltpu.VMEM((NCH, NX, NZ, CB, 8, BLOCK), BF),
        zacc=pltpu.VMEM((NCH, NZ, CB, 8, BLOCK), F32),
        zs=pltpu.VMEM((NCH, NZ, CB, 8, BLOCK), BF),
        zr=pltpu.VMEM((NCH, NZ, CB, 8, BLOCK), BF),
        sol=pltpu.VMEM((sz.NB, 8, BLOCK), BF),
        ysd=pltpu.VMEM((NY, CAP, 8, BLOCK), BF),
        yrc=pltpu.VMEM((NY, CAP, 8, BLOCK), BF),
        gath=pltpu.VMEM((Q, G, 8, BLOCK), BF),
        lhs=pltpu.VMEM((sz.C, sz.U), BF),
        ycs=pltpu.VMEM((NY, sz.CY, sz.S3), F32),
        y1s=pltpu.VMEM((NY, sz.CY, sz.S3), BF),
        ycr=pltpu.VMEM((NY, sz.CY, sz.S3), BF),
        red=pltpu.VMEM((NY, sz.CY, sz.S3), BF),
        o1=pltpu.VMEM((NZ, sz.SPAN, 8, BLOCK), BF),
        o2=pltpu.VMEM((NX, NZ, sz.SPAN, 8, BLOCK), BF),
        ot=pltpu.VMEM((sz.SPAN * BLOCK, sz.C), F32),
        p5f=pltpu.VMEM((NZ, NX, sz.TC, sz.C), F32),
        p5s=pltpu.VMEM((NZ, NX, sz.TC, sz.C), BF),
        p5r=pltpu.VMEM((NZ, NX, sz.TC, sz.C), BF),
        z5s=pltpu.VMEM((NZ, sz.TC, sz.C), BF),
        z5r=pltpu.VMEM((NZ, sz.TC, sz.C), BF),
        sel=pltpu.SMEM((NY * CAP,), jnp.int32),
        pos=pltpu.SMEM((G,), jnp.int32),
        lsem=pltpu.SemaphoreType.DMA((4,)),
        csem=dma(NCH),
        xsem=dma(NCH, NX),
        zsem=dma(NCH, NZ),
        c2sem=dma(1),
        ysem=dma(NY),
        o1sem=dma(NZ),
        o2sem=dma(NX),
        agx=dma(NX),
        agu=dma(NX, NZ // 2 + 1),
        agd=dma(NX, NZ // 2 + 1),
        y1sem=dma(NY),
        y2sem=dma(NY),
        p5sem=dma(NZ, NX),
        z5sem=dma(NZ),
    )
    names = list(scratch)

    def body(*refs):
        kernel(sz, *refs[:9], **dict(zip(names, refs[9:])))

    return pl.pallas_call(
        body,
        name="backward",
        out_shape=(
            jax.ShapeDtypeStruct((sz.TO, sz.C), BF),
            jax.ShapeDtypeStruct((1, sz.TC, sz.C), BF),
        ),
        in_specs=[vmem, hbm, vmem, hbm, hbm, smem, smem],
        out_specs=(vmem, vmem),
        scratch_shapes=list(scratch.values()),
        compiler_params=pltpu.CompilerParams(
            collective_id=0, has_side_effects=True, vmem_limit_bytes=56 * 1024 * 1024
        ),
    )(root_rhs, root_inverse, child_rhs, child_inverse, coupling, block_map, block_count)


def solution(mesh):
    in_specs = (
        P(("col", "cores"), None),
        P(("col", "cores"), "row"),
        P("cores", "col", None),
        P("cores", "col", "row"),
        P("cores", "row", "col"),
        P(),
        P(),
    )
    out_specs = (P(("row", "col", "cores"), None), P("cores", ("row", "col"), None))
    return jax.shard_map(
        functools.partial(per_device, mesh),
        mesh=mesh, in_specs=in_specs, out_specs=out_specs, check_vma=False,
    )
```

```python
import functools

import jax
import jax.numpy as jnp
from jax import lax
from jax.experimental import pallas as pl
from jax.experimental.pallas import tpu as pltpu
from jax.sharding import PartitionSpec as P

BLOCK = 128
CAP = 3
GRID = {32: (4, 8), 4: (2, 2)}
MESH = pl.DeviceIdType.MESH
BF = jnp.bfloat16
F32 = jnp.float32


class Sizes:
    def __init__(self, mesh, root_rhs, root_inverse, child_inverse, coupling):
        self.NY = mesh.shape["row"]
        self.NX, self.NZ = GRID[mesh.shape["col"]]
        self.Q = self.NX * self.NZ
        self.S1, self.C = root_rhs.shape
        self.T1 = root_inverse.shape[1]
        self.NB = self.T1 // BLOCK
        self.HB = self.NB // 2
        self.S3, self.T3 = child_inverse.shape[1:]
        self.U = coupling.shape[1]
        self.G = self.U // BLOCK
        self.HA = max(self.G // 5, 1)
        self.CY = self.C // self.NY
        self.TO = self.T1 // (2 * self.Q)
        self.TC = self.T3 // self.Q
        self.TZ = self.T1 // self.NZ
        self.AB = max(8 * self.HB // 10, 1)
        self.RA = self.TC - 8
        starts = [self.TZ * z // BLOCK for z in range(self.NZ)]
        ends = [-(-self.TZ * (z + 1) // BLOCK) for z in range(self.NZ)]
        self.SPAN = max(e - s for s, e in zip(starts, ends))
        self.full = self.S3 // BLOCK
        self.packed = (self.CY * self.S3 // BLOCK, BLOCK)

    def pack(self, v):
        h = self.CY // 2
        parts = [v[:, i * BLOCK:(i + 1) * BLOCK] for i in range(self.full)]
        if self.S3 % BLOCK:
            rest = v[:, self.full * BLOCK:]
            parts.append(jnp.concatenate([rest[:h], rest[h:]], axis=1))
        return jnp.concatenate(parts, axis=0)

    def unpack(self, v):
        h, n = self.CY // 2, self.CY
        parts = [v[i * n:(i + 1) * n] for i in range(self.full)]
        if self.S3 % BLOCK:
            rest = v[self.full * n:]
            parts.append(jnp.concatenate([rest[:, :BLOCK // 2], rest[:, BLOCK // 2:]], axis=0))
        return jnp.concatenate(parts, axis=1)


def far_first(n):
    return sorted(range(1, n), key=lambda d: (-min(d, n - d), d))


def kernel(
    sz, rrhs, rinv, crhs, cinv, coup, bmap, bcnt, out, *,
    rrhs_v, rinv_v, crhs_v, coup_v, cinv_v, bmap_s, bcnt_s, cit, rhs_t, crhs_t, cs, cr, own, xs, xr, zs, zr, ws, wr, ts, tr, sol,
    ysd, yrc, ga, gb, lhs, ycs, y1s, ycr, red, red_s, o1, o2, ot, p5f, p5s, p5r, z5s, z5r, w5s, w5r, t5s, t5r, sel, pos,
    lsem, csem, xsem, zsem, wsem, tsem, c2sem, ysem, o1sem, o2sem, agx, aga, agz, agc, y1sem, y2sem, p5sem, z5sem, w5sem, t5sem,
):
    NX, NZ, NY, HB, NB, G, HA = sz.NX, sz.NZ, sz.NY, sz.HB, sz.NB, sz.G, sz.HA
    r, c, k = lax.axis_index("row"), lax.axis_index("col"), lax.axis_index("cores")
    z, x = c // NX, lax.rem(c, NX)
    AB, RA = sz.AB, sz.RA

    def xd(d):
        return lax.rem(x + d + NX, NX)

    def zd(d):
        return lax.rem(z + d + NZ, NZ)

    def yd(d):
        return lax.rem(r + d + NY, NY)

    def dev_x(d):
        return (r, z * NX + xd(d), k)

    def dev_z(d):
        return (r, zd(d) * NX + x, k)

    def dev_y(d):
        return (yd(d), c, k)

    def near(i):
        if isinstance(i, int):
            return NZ - (i + 1) // 2 if i % 2 else i // 2
        return jnp.where(lax.rem(i, 2) == 1, NZ - (i + 1) // 2, i // 2)

    dev_c = (r, c, 1 - k)
    sent = []

    def send(src, dst, sem, idx, dev, to=None):
        cp = pltpu.make_async_remote_copy(
            src_ref=src, dst_ref=dst, send_sem=sem.at[(0,) + idx], recv_sem=sem.at[(1,) + (to or idx)],
            device_id=dev, device_id_type=MESH,
        )
        cp.start()
        sent.append(cp)

    def drain():
        for cp in sent:
            cp.wait_send()
        sent.clear()

    def arrived(ref, sem, idx):
        pltpu.make_async_remote_copy(
            src_ref=ref, dst_ref=ref, send_sem=sem.at[(0,) + idx], recv_sem=sem.at[(1,) + idx],
            device_id=dev_c, device_id_type=MESH,
        ).wait_recv()

    half = HB * BLOCK
    theirs = pl.ds(pl.multiple_of((1 - k) * half, BLOCK), half)
    ours = pl.ds(pl.multiple_of(k * half, BLOCK), half)
    pairs = [
        (rrhs, rrhs_v), (rinv.at[:, theirs], rinv_v.at[:, theirs]), (rinv.at[:, ours], rinv_v.at[:, ours]),
        (bmap, bmap_s), (bcnt, bcnt_s), (cinv.at[0], cinv_v), (crhs.at[0], crhs_v), (coup.at[0], coup_v),
    ]
    loads = [pltpu.make_async_copy(a, b, lsem.at[i]) for i, (a, b) in enumerate(pairs)]
    for cp in loads:
        cp.start()
    load_rrhs, load_theirs, load_ours, load_map, load_count, load_cinv, load_crhs, load_coup = loads

    barrier = pltpu.get_barrier_semaphore()
    peers = (
        [dev_c]
        + [dev_x(d) for d in range(1, NX)]
        + [dev_z(d) for d in range(1, NZ)]
        + [dev_y(d) for d in range(1, NY)]
    )
    for dev in peers:
        pl.semaphore_signal(barrier, inc=1, device_id=dev, device_id_type=MESH)

    def partial(which, dst):
        for b in range(0, HB, 2):
            off = pl.multiple_of(which * half + b * BLOCK, BLOCK)
            v = jnp.dot(rhs_t[...], rinv_v[:, pl.ds(off, 2 * BLOCK)], preferred_element_type=F32)
            for i in range(2):
                dst[:, :, b + i] = v[:, i * BLOCK:(i + 1) * BLOCK].reshape(NZ, NX, 8, BLOCK)

    order = far_first(NZ) + [0]
    load_rrhs.wait()
    rhs_t[...] = rrhs_v[...].astype(F32).T.astype(BF)
    load_theirs.wait()
    partial(1 - k, cs)
    load_ours.wait()
    partial(k, own)
    pl.semaphore_wait(barrier, len(peers))
    for d in order:
        send(cs.at[zd(d)], cr.at[zd(d)], csem, (d,), dev_c)

    for d in order:
        arrived(cr.at[zd(d)], csem, (d,))
        if d:
            ws[d] = (own[zd(d), :, AB:] + cr[zd(d), :, AB:]).astype(BF)
            send(ws.at[d], wr.at[d], wsem, (d,), dev_z(d), to=(0,))
        for e in range(1, NX):
            xs[d, e] = (own[zd(d), xd(e), :AB] + cr[zd(d), xd(e), :AB]).astype(BF)
            send(xs.at[d, e], xr.at[d, e], xsem, (d, e), dev_x(e), to=(d, 0))
    for d in order:
        acc = own[zd(d), x, :AB] + cr[zd(d), x, :AB]
        arrived(xr.at[d, pl.ds(1, NX - 1)], xsem, (d, 0))
        for e in range(1, NX):
            acc = acc + xr[d, e].astype(F32)
        if d:
            zs[d] = acc.astype(BF)
            send(zs.at[d], zr.at[d], zsem, (d,), dev_z(d))
        else:
            own[z, x, :AB] = acc
    acc = own[z, :, AB:] + cr[z, :, AB:]
    arrived(wr.at[pl.ds(1, NZ - 1)], wsem, (0,))
    for d in range(1, NZ):
        acc = acc + wr[d].astype(F32)
    own[z, :, AB:] = acc
    for e in range(1, NX):
        ts[e] = own[z, xd(e), AB:].astype(BF)
        send(ts.at[e], tr.at[e], tsem, (e,), dev_x(e), to=(0,))

    def choose(t, _):
        cnt = jnp.int32(0)
        got = [jnp.int32(0)] * CAP
        for s in range(G):
            b = bmap_s[k, t * G + s] - r * NB
            inside = jnp.logical_and(b >= 0, b < NB)
            for j in range(CAP):
                got[j] = jnp.where(jnp.logical_and(inside, cnt == j), b, got[j])
            cnt = cnt + jnp.where(inside, 1, 0)
        for j in range(CAP):
            sel[t * CAP + j] = got[j]
        return 0

    load_map.wait()
    load_count.wait()
    lax.fori_loop(0, NY, choose, 0)

    acc = own[z, x, :AB]
    for d in far_first(NZ):
        arrived(zr.at[d], zsem, (d,))
        acc = acc + zr[d].astype(F32)
    sol[pl.ds(k * HB, AB)] = acc.astype(BF)
    acc = own[z, x, AB:]
    arrived(tr.at[pl.ds(1, NX - 1)], tsem, (0,))
    for e in range(1, NX):
        acc = acc + tr[e].astype(F32)
    sol[pl.ds(k * HB + AB, HB - AB)] = acc.astype(BF)
    mine = pl.ds(k * HB, HB)
    send(sol.at[mine], sol.at[mine], c2sem, (0,), dev_c)
    arrived(sol.at[pl.ds((1 - k) * HB, HB)], c2sem, (0,))

    for d in far_first(NY) + [0]:
        t = yd(d)
        for j in range(CAP):
            v = sol[sel[t * CAP + j]]
            if d:
                ysd[d, j] = v
            else:
                yrc[r * CAP + j] = v
        if d:
            send(ysd.at[d], yrc.at[pl.ds(r * CAP, CAP)], ysem, (d,), dev_y(d))

    ranges = [lax.div(bmap_s[k, r * G + s], jnp.int32(NB)) for s in range(G)]
    for s in range(G):
        rank = jnp.int32(0)
        for e in range(s):
            rank = rank + jnp.where(ranges[e] == ranges[s], 1, 0)
        pos[s] = ranges[s] * CAP + jnp.minimum(rank, CAP - 1)
    drain()
    for d in range(1, NY):
        arrived(yrc.at[pl.ds(yd(-d) * CAP, CAP)], ysem, (d,))
    for s in [*range(HA, G), *range(HA)]:
        v = yrc[pos[s]]
        alive = r * G + s < bcnt_s[k]
        v = jnp.where(alive, v.astype(F32), 0.0).astype(BF)
        if s < HA:
            ga[0, 0, s] = v
        else:
            gb[0, 0, s - HA] = v

    for e in range(1, NX):
        send(ga.at[0, 0], ga.at[0, e], agx, (e,), dev_x(e))
    for i in range(1, NZ):
        send(gb.at[0, 0], gb.at[0, i], agz, (i,), dev_z(near(i)))

    def spread(i):
        for e in range(1, NX):
            send(gb.at[0, i], gb.at[e, i], agc, (e, i), dev_x(e), to=(e, 0))

    spread(0)
    for e in range(1, NX):
        arrived(ga.at[0, e], agx, (e,))
    for i in range(1, NZ):
        send(ga.at[0], ga.at[i], aga, (i,), dev_z(near(i)))
    for i in range(1, NZ):
        arrived(gb.at[0, i], agz, (i,))
        spread(i)
    load_coup.wait()

    for i in range(1, NZ):
        arrived(ga.at[i], aga, (i,))
    for s in range(HA):
        lhs[:, s * BLOCK:(s + 1) * BLOCK] = ga[:, :, s].reshape(sz.C, BLOCK)
    for e in range(1, NX):
        arrived(gb.at[e], agc, (e, 0))
    for s in range(HA, G):
        v = jnp.stack([gb[e, :, s - HA] for e in range(NX)], axis=1)
        lhs[:, s * BLOCK:(s + 1) * BLOCK] = v.reshape(sz.C, BLOCK)
    prod = lax.dot_general(lhs[...], coup_v[...], (((1,), (1,)), ((), ())), preferred_element_type=F32)
    for t in range(NY):
        ycs[t] = sz.pack(prod[t * sz.CY:(t + 1) * sz.CY, :])
    for d in far_first(NY):
        y1s[d] = ycs[yd(d)].astype(BF)
        send(y1s.at[d], ycr.at[d], y1sem, (d,), dev_y(d))

    def first_block(zz):
        return (sz.TZ * zz) // BLOCK

    for d in far_first(NZ):
        send(sol.at[pl.ds(first_block(zd(d)), sz.SPAN)], o1.at[z], o1sem, (d,), dev_z(d))
    o1[z] = sol[pl.ds(first_block(z), sz.SPAN)]

    load_crhs.wait()
    crhs_t[...] = crhs_v[...].astype(F32).T
    load_cinv.wait()
    for j in range(sz.T3 // BLOCK):
        cols = slice(j * BLOCK, (j + 1) * BLOCK)
        cit[cols, :] = cinv_v[:, cols].astype(F32).T.astype(BF)

    acc = ycs[r]
    for d in far_first(NY)[::-1]:
        arrived(ycr.at[d], y1sem, (d,))
        acc = acc + ycr[d].astype(F32)
    acc = sz.unpack(acc)
    from_z = zd(-near(r))
    diff = []
    for e in range(NX):
        rows = pl.ds(pl.multiple_of((from_z * NX + xd(-e)) * 8, 8), 8)
        diff.append(crhs_t[rows, :] - acc[e * 8:(e + 1) * 8, :])
    red[0] = sz.pack(jnp.concatenate(diff, axis=0)).astype(BF)
    for d in far_first(NY):
        send(red.at[0], red.at[d], y2sem, (d,), dev_y(d))

    for d in range(1, NZ):
        arrived(o1.at[zd(-d)], o1sem, (d,))
    for d in range(1, NX):
        send(o1, o2.at[x], o2sem, (d,), dev_x(d))
    o2[x] = o1[...]
    drain()
    for d in range(1, NX):
        arrived(o2.at[xd(-d)], o2sem, (d,))
    for b in range(sz.SPAN):
        v = jnp.stack([o2[e, :, b] for e in range(NX)], axis=1)
        ot[b * BLOCK:(b + 1) * BLOCK, :] = v.astype(F32).reshape(sz.C, BLOCK).T
    first_row = sz.TZ * z + (2 * x + k) * sz.TO - first_block(z) * BLOCK
    out[:sz.TO] = ot[pl.ds(pl.multiple_of(first_row, 8), sz.TO), :].astype(BF)

    for d in range(1, NY):
        arrived(red.at[d], y2sem, (d,))
    for d in range(NY):
        v = sz.unpack(red[d].astype(F32)).astype(BF).reshape(NX, 8, sz.S3)
        for e in range(NX):
            red_s[zd(-near(yd(-d))), xd(-e)] = v[e]
    reduced = red_s[...].reshape(sz.C, sz.S3)
    rows_z = NX * sz.TC
    for d in order:
        rows = pl.ds(pl.multiple_of(zd(d) * rows_z, rows_z), rows_z)
        v = lax.dot_general(cit[rows, :], reduced, (((1,), (1,)), ((), ())), preferred_element_type=F32)
        p5f[d] = v.reshape(NX, sz.TC, sz.C)
        if d:
            w5s[d] = p5f[d, :, RA:].astype(BF)
            send(w5s.at[d], w5r.at[d], w5sem, (d,), dev_z(d), to=(0,))
        for e in range(1, NX):
            p5s[d, e] = p5f[d, xd(e), :RA].astype(BF)
            send(p5s.at[d, e], p5r.at[d, e], p5sem, (d, e), dev_x(e), to=(d, 0))
    for d in order:
        acc = p5f[d, x, :RA]
        arrived(p5r.at[d, pl.ds(1, NX - 1)], p5sem, (d, 0))
        for e in range(1, NX):
            acc = acc + p5r[d, e].astype(F32)
        if d:
            z5s[d] = acc.astype(BF)
            send(z5s.at[d], z5r.at[d], z5sem, (d,), dev_z(d))
    p5f[0, x, :RA] = acc
    acc = p5f[0, :, RA:]
    arrived(w5r.at[pl.ds(1, NZ - 1)], w5sem, (0,))
    for d in range(1, NZ):
        acc = acc + w5r[d].astype(F32)
    p5f[0, :, RA:] = acc
    for e in range(1, NX):
        t5s[e] = p5f[0, xd(e), RA:].astype(BF)
        send(t5s.at[e], t5r.at[e], t5sem, (e,), dev_x(e), to=(0,))
    drain()
    acc = p5f[0, x, :RA]
    for d in far_first(NZ):
        arrived(z5r.at[d], z5sem, (d,))
        acc = acc + z5r[d].astype(F32)
    out[sz.TO:sz.TO + RA] = acc.astype(BF)
    acc = p5f[0, x, RA:]
    arrived(t5r.at[pl.ds(1, NX - 1)], t5sem, (0,))
    for e in range(1, NX):
        acc = acc + t5r[e].astype(F32)
    out[sz.TO + RA:] = acc.astype(BF)


def per_device(mesh, root_rhs, root_inverse, child_rhs, child_inverse, coupling, block_map, block_count):
    sz = Sizes(mesh, root_rhs, root_inverse, child_inverse, coupling)
    coupling = jnp.swapaxes(coupling, 1, 2)
    NX, NZ, NY, HB, Q, G, HA = sz.NX, sz.NZ, sz.NY, sz.HB, sz.Q, sz.G, sz.HA
    AB, RA = sz.AB, sz.RA
    vmem = pl.BlockSpec(memory_space=pltpu.VMEM)
    hbm = pl.BlockSpec(memory_space=pl.ANY)

    def dma(*shape):
        return pltpu.SemaphoreType.DMA((2,) + shape)

    scratch = dict(
        rrhs_v=pltpu.VMEM((sz.S1, sz.C), BF),
        rinv_v=pltpu.VMEM((sz.S1, sz.T1), BF),
        crhs_v=pltpu.VMEM((sz.S3, sz.C), BF),
        coup_v=pltpu.VMEM((sz.S3, sz.U), BF),
        cinv_v=pltpu.VMEM((sz.S3, sz.T3), BF),
        bmap_s=pltpu.SMEM(block_map.shape, jnp.int32),
        bcnt_s=pltpu.SMEM(block_count.shape, jnp.int32),
        cit=pltpu.VMEM((sz.T3, sz.S3), BF),
        rhs_t=pltpu.VMEM((sz.C, sz.S1), BF),
        crhs_t=pltpu.VMEM((sz.C, sz.S3), F32),
        cs=pltpu.VMEM((NZ, NX, HB, 8, BLOCK), F32),
        cr=pltpu.VMEM((NZ, NX, HB, 8, BLOCK), F32),
        own=pltpu.VMEM((NZ, NX, HB, 8, BLOCK), F32),
        xs=pltpu.VMEM((NZ, NX, AB, 8, BLOCK), BF),
        xr=pltpu.VMEM((NZ, NX, AB, 8, BLOCK), BF),
        zs=pltpu.VMEM((NZ, AB, 8, BLOCK), BF),
        zr=pltpu.VMEM((NZ, AB, 8, BLOCK), BF),
        ws=pltpu.VMEM((NZ, NX, HB - AB, 8, BLOCK), BF),
        wr=pltpu.VMEM((NZ, NX, HB - AB, 8, BLOCK), BF),
        ts=pltpu.VMEM((NX, HB - AB, 8, BLOCK), BF),
        tr=pltpu.VMEM((NX, HB - AB, 8, BLOCK), BF),
        sol=pltpu.VMEM((sz.NB, 8, BLOCK), BF),
        ysd=pltpu.VMEM((NY, CAP, 8, BLOCK), BF),
        yrc=pltpu.VMEM((NY * CAP, 8, BLOCK), BF),
        ga=pltpu.VMEM((NZ, NX, HA, 8, BLOCK), BF),
        gb=pltpu.VMEM((NX, NZ, G - HA, 8, BLOCK), BF),
        lhs=pltpu.VMEM((sz.C, sz.U), BF),
        ycs=pltpu.VMEM((NY,) + sz.packed, F32),
        y1s=pltpu.VMEM((NY,) + sz.packed, BF),
        ycr=pltpu.VMEM((NY,) + sz.packed, BF),
        red=pltpu.VMEM((NY,) + sz.packed, BF),
        red_s=pltpu.VMEM((NZ, NX, 8, sz.S3), BF),
        o1=pltpu.VMEM((NZ, sz.SPAN, 8, BLOCK), BF),
        o2=pltpu.VMEM((NX, NZ, sz.SPAN, 8, BLOCK), BF),
        ot=pltpu.VMEM((sz.SPAN * BLOCK, sz.C), F32),
        p5f=pltpu.VMEM((NZ, NX, sz.TC, sz.C), F32),
        p5s=pltpu.VMEM((NZ, NX, RA, sz.C), BF),
        p5r=pltpu.VMEM((NZ, NX, RA, sz.C), BF),
        z5s=pltpu.VMEM((NZ, RA, sz.C), BF),
        z5r=pltpu.VMEM((NZ, RA, sz.C), BF),
        w5s=pltpu.VMEM((NZ, NX, sz.TC - RA, sz.C), BF),
        w5r=pltpu.VMEM((NZ, NX, sz.TC - RA, sz.C), BF),
        t5s=pltpu.VMEM((NX, sz.TC - RA, sz.C), BF),
        t5r=pltpu.VMEM((NX, sz.TC - RA, sz.C), BF),
        sel=pltpu.SMEM((NY * CAP,), jnp.int32),
        pos=pltpu.SMEM((G,), jnp.int32),
        lsem=pltpu.SemaphoreType.DMA((8,)),
        csem=dma(NZ),
        xsem=dma(NZ, NX),
        zsem=dma(NZ),
        wsem=dma(NZ),
        tsem=dma(NX),
        c2sem=dma(1),
        ysem=dma(NY),
        o1sem=dma(NZ),
        o2sem=dma(NX),
        agx=dma(NX),
        aga=dma(NZ),
        agz=dma(NZ),
        agc=dma(NX, NZ),
        y1sem=dma(NY),
        y2sem=dma(NY),
        p5sem=dma(NZ, NX),
        z5sem=dma(NZ),
        w5sem=dma(NZ),
        t5sem=dma(NX),
    )
    names = list(scratch)

    def body(*refs):
        kernel(sz, *refs[:8], **dict(zip(names, refs[8:])))

    both = pl.pallas_call(
        body,
        name="backward",
        out_shape=jax.ShapeDtypeStruct((sz.TO + sz.TC, sz.C), BF),
        in_specs=[hbm] * 7,
        out_specs=vmem,
        scratch_shapes=list(scratch.values()),
        compiler_params=pltpu.CompilerParams(
            collective_id=0, has_side_effects=True, vmem_limit_bytes=56 * 1024 * 1024
        ),
    )(root_rhs, root_inverse, child_rhs, child_inverse, coupling, block_map, block_count)
    return both[:sz.TO], both[sz.TO:][None]


def solution(mesh):
    in_specs = (
        P(("col", "cores"), None),
        P(("col", "cores"), "row"),
        P("cores", "col", None),
        P("cores", "col", "row"),
        P("cores", "row", "col"),
        P(),
        P(),
    )
    out_specs = (P(("row", "col", "cores"), None), P("cores", ("row", "col"), None))
    return jax.shard_map(
        functools.partial(per_device, mesh),
        mesh=mesh, in_specs=in_specs, out_specs=out_specs, check_vma=False,
    )
```

```python
import functools

import jax
import jax.numpy as jnp
from jax import lax
from jax.experimental import pallas as pl
from jax.experimental.pallas import tpu as pltpu
from jax.sharding import PartitionSpec as P

BLOCK = 128
CAP = 3
GRID = {32: (4, 8), 4: (2, 2)}
MESH = pl.DeviceIdType.MESH
BF = jnp.bfloat16
F32 = jnp.float32


class Sizes:
    def __init__(self, mesh, root_rhs, root_inverse, child_inverse, coupling):
        self.NY = mesh.shape["row"]
        self.NX, self.NZ = GRID[mesh.shape["col"]]
        self.Q = self.NX * self.NZ
        self.S1, self.C = root_rhs.shape
        self.T1 = root_inverse.shape[1]
        self.NB = self.T1 // BLOCK
        self.HB = self.NB // 2
        self.S3, self.T3 = child_inverse.shape[1:]
        self.U = coupling.shape[1]
        self.G = self.U // BLOCK
        self.HA = max(self.G // 5, 1)
        self.CY = self.C // self.NY
        self.TO = self.T1 // (2 * self.Q)
        self.TC = self.T3 // self.Q
        self.TZ = self.T1 // self.NZ
        self.AB = max(8 * self.HB // 10, 1)
        self.RA = self.TC - 8
        starts = [self.TZ * z // BLOCK for z in range(self.NZ)]
        ends = [-(-self.TZ * (z + 1) // BLOCK) for z in range(self.NZ)]
        self.SPAN = max(e - s for s, e in zip(starts, ends))
        self.full = self.S3 // BLOCK
        self.packed = (self.CY * self.S3 // BLOCK, BLOCK)

    def pack(self, v):
        h = self.CY // 2
        parts = [v[:, i * BLOCK:(i + 1) * BLOCK] for i in range(self.full)]
        if self.S3 % BLOCK:
            rest = v[:, self.full * BLOCK:]
            parts.append(jnp.concatenate([rest[:h], rest[h:]], axis=1))
        return jnp.concatenate(parts, axis=0)

    def unpack(self, v):
        h, n = self.CY // 2, self.CY
        parts = [v[i * n:(i + 1) * n] for i in range(self.full)]
        if self.S3 % BLOCK:
            rest = v[self.full * n:]
            parts.append(jnp.concatenate([rest[:, :BLOCK // 2], rest[:, BLOCK // 2:]], axis=0))
        return jnp.concatenate(parts, axis=1)


def far_first(n):
    return sorted(range(1, n), key=lambda d: (-min(d, n - d), d))


def kernel(
    sz, rrhs, rinv, crhs, cinv, coup, bmap, bcnt, out, *,
    rrhs_v, rinv_v, crhs_v, coup_v, cinv_v, bmap_s, bcnt_s, cit, rhs_t, crhs_t, cs, cr, own, xs, xr, zs, zr, ws, wr, ts, tr, sol,
    ysd, yrc, ga, gb, lhs, ycs, y1s, ycr, red, red_s, o1, o2, ot, p5f, p5s, p5r, z5s, z5r, w5s, w5r, t5s, t5r, sel, pos,
    lsem, csem, xsem, zsem, wsem, tsem, c2sem, ysem, o1sem, o2sem, agx, aga, agz, agc, y1sem, y2sem, p5sem, z5sem, w5sem, t5sem,
):
    NX, NZ, NY, HB, NB, G, HA = sz.NX, sz.NZ, sz.NY, sz.HB, sz.NB, sz.G, sz.HA
    r, c, k = lax.axis_index("row"), lax.axis_index("col"), lax.axis_index("cores")
    z, x = c // NX, lax.rem(c, NX)
    AB, RA = sz.AB, sz.RA

    def xd(d):
        return lax.rem(x + d + NX, NX)

    def zd(d):
        return lax.rem(z + d + NZ, NZ)

    def yd(d):
        return lax.rem(r + d + NY, NY)

    def dev_x(d):
        return (r, z * NX + xd(d), k)

    def dev_z(d):
        return (r, zd(d) * NX + x, k)

    def dev_y(d):
        return (yd(d), c, k)

    def near(i):
        if isinstance(i, int):
            return NZ - (i + 1) // 2 if i % 2 else i // 2
        return jnp.where(lax.rem(i, 2) == 1, NZ - (i + 1) // 2, i // 2)

    dev_c = (r, c, 1 - k)
    sent = []

    def send(src, dst, sem, idx, dev, to=None):
        cp = pltpu.make_async_remote_copy(
            src_ref=src, dst_ref=dst, send_sem=sem.at[(0,) + idx], recv_sem=sem.at[(1,) + (to or idx)],
            device_id=dev, device_id_type=MESH,
        )
        cp.start()
        sent.append(cp)

    def drain():
        for cp in sent:
            cp.wait_send()
        sent.clear()

    def arrived(ref, sem, idx):
        pltpu.make_async_remote_copy(
            src_ref=ref, dst_ref=ref, send_sem=sem.at[(0,) + idx], recv_sem=sem.at[(1,) + idx],
            device_id=dev_c, device_id_type=MESH,
        ).wait_recv()

    half = HB * BLOCK
    theirs = pl.ds(pl.multiple_of((1 - k) * half, BLOCK), half)
    ours = pl.ds(pl.multiple_of(k * half, BLOCK), half)
    pairs = [
        (rrhs, rrhs_v), (rinv.at[:, theirs], rinv_v.at[:, theirs]), (rinv.at[:, ours], rinv_v.at[:, ours]),
        (bmap, bmap_s), (bcnt, bcnt_s), (cinv.at[0], cinv_v), (crhs.at[0], crhs_v), (coup.at[0], coup_v),
    ]
    loads = [pltpu.make_async_copy(a, b, lsem.at[i]) for i, (a, b) in enumerate(pairs)]
    for cp in loads[:3]:
        cp.start()
    load_rrhs, load_theirs, load_ours, load_map, load_count, load_cinv, load_crhs, load_coup = loads

    barrier = pltpu.get_barrier_semaphore()
    peers = (
        [dev_c]
        + [dev_x(d) for d in range(1, NX)]
        + [dev_z(d) for d in range(1, NZ)]
        + [dev_y(d) for d in range(1, NY)]
    )
    for dev in peers:
        pl.semaphore_signal(barrier, inc=1, device_id=dev, device_id_type=MESH)

    def partial(which, dst):
        for b in range(0, HB, 2):
            off = pl.multiple_of(which * half + b * BLOCK, BLOCK)
            v = jnp.dot(rhs_t[...], rinv_v[:, pl.ds(off, 2 * BLOCK)], preferred_element_type=F32)
            for i in range(2):
                dst[:, :, b + i] = v[:, i * BLOCK:(i + 1) * BLOCK].reshape(NZ, NX, 8, BLOCK)

    order = far_first(NZ) + [0]
    load_rrhs.wait()
    rhs_t[...] = rrhs_v[...].astype(F32).T.astype(BF)
    load_theirs.wait()
    partial(1 - k, cs)
    load_ours.wait()
    partial(k, own)
    for cp in loads[3:]:
        cp.start()
    pl.semaphore_wait(barrier, len(peers))
    for d in order:
        send(cs.at[zd(d)], cr.at[zd(d)], csem, (d,), dev_c)

    for d in order:
        arrived(cr.at[zd(d)], csem, (d,))
        if d:
            ws[d] = (own[zd(d), :, AB:] + cr[zd(d), :, AB:]).astype(BF)
            send(ws.at[d], wr.at[d], wsem, (d,), dev_z(d), to=(0,))
        for e in far_first(NX):
            xs[d, e] = (own[zd(d), xd(e), :AB] + cr[zd(d), xd(e), :AB]).astype(BF)
            send(xs.at[d, e], xr.at[d, e], xsem, (d, e), dev_x(e), to=(d, 0))
    for d in order:
        acc = own[zd(d), x, :AB] + cr[zd(d), x, :AB]
        arrived(xr.at[d, pl.ds(1, NX - 1)], xsem, (d, 0))
        for e in range(1, NX):
            acc = acc + xr[d, e].astype(F32)
        if d:
            zs[d] = acc.astype(BF)
            send(zs.at[d], zr.at[d], zsem, (d,), dev_z(d))
        else:
            own[z, x, :AB] = acc
    acc = own[z, :, AB:] + cr[z, :, AB:]
    arrived(wr.at[pl.ds(1, NZ - 1)], wsem, (0,))
    for d in range(1, NZ):
        acc = acc + wr[d].astype(F32)
    own[z, :, AB:] = acc
    for e in far_first(NX):
        ts[e] = own[z, xd(e), AB:].astype(BF)
        send(ts.at[e], tr.at[e], tsem, (e,), dev_x(e), to=(0,))

    def choose(t, _):
        cnt = jnp.int32(0)
        got = [jnp.int32(0)] * CAP
        for s in range(G):
            b = bmap_s[k, t * G + s] - r * NB
            inside = jnp.logical_and(b >= 0, b < NB)
            for j in range(CAP):
                got[j] = jnp.where(jnp.logical_and(inside, cnt == j), b, got[j])
            cnt = cnt + jnp.where(inside, 1, 0)
        for j in range(CAP):
            sel[t * CAP + j] = got[j]
        return 0

    load_map.wait()
    load_count.wait()
    lax.fori_loop(0, NY, choose, 0)

    acc = own[z, x, :AB]
    for d in far_first(NZ):
        arrived(zr.at[d], zsem, (d,))
        acc = acc + zr[d].astype(F32)
    sol[pl.ds(k * HB, AB)] = acc.astype(BF)
    acc = own[z, x, AB:]
    arrived(tr.at[pl.ds(1, NX - 1)], tsem, (0,))
    for e in range(1, NX):
        acc = acc + tr[e].astype(F32)
    sol[pl.ds(k * HB + AB, HB - AB)] = acc.astype(BF)
    mine = pl.ds(k * HB, HB)
    send(sol.at[mine], sol.at[mine], c2sem, (0,), dev_c)
    arrived(sol.at[pl.ds((1 - k) * HB, HB)], c2sem, (0,))

    for d in far_first(NY) + [0]:
        t = yd(d)
        for j in range(CAP):
            v = sol[sel[t * CAP + j]]
            if d:
                ysd[d, j] = v
            else:
                yrc[r * CAP + j] = v
        if d:
            send(ysd.at[d], yrc.at[pl.ds(r * CAP, CAP)], ysem, (d,), dev_y(d))

    ranges = [lax.div(bmap_s[k, r * G + s], jnp.int32(NB)) for s in range(G)]
    for s in range(G):
        rank = jnp.int32(0)
        for e in range(s):
            rank = rank + jnp.where(ranges[e] == ranges[s], 1, 0)
        pos[s] = ranges[s] * CAP + jnp.minimum(rank, CAP - 1)
    drain()
    for d in range(1, NY):
        arrived(yrc.at[pl.ds(yd(-d) * CAP, CAP)], ysem, (d,))
    for s in [*range(HA, G), *range(HA)]:
        v = yrc[pos[s]]
        alive = r * G + s < bcnt_s[k]
        v = jnp.where(alive, v.astype(F32), 0.0).astype(BF)
        if s < HA:
            ga[0, 0, s] = v
        else:
            gb[0, 0, s - HA] = v

    for e in far_first(NX):
        send(ga.at[0, 0], ga.at[0, e], agx, (e,), dev_x(e))
    for i in range(1, NZ):
        send(gb.at[0, 0], gb.at[0, i], agz, (i,), dev_z(near(i)))

    def spread(i):
        for e in range(1, NX):
            send(gb.at[0, i], gb.at[e, i], agc, (e, i), dev_x(e), to=(e, 0))

    spread(0)
    for e in range(1, NX):
        arrived(ga.at[0, e], agx, (e,))
    for i in range(1, NZ):
        send(ga.at[0], ga.at[i], aga, (i,), dev_z(near(i)))
    for i in range(1, NZ):
        arrived(gb.at[0, i], agz, (i,))
        spread(i)
    load_coup.wait()

    for i in range(1, NZ):
        arrived(ga.at[i], aga, (i,))
    for s in range(HA):
        lhs[:, s * BLOCK:(s + 1) * BLOCK] = ga[:, :, s].reshape(sz.C, BLOCK)
    for e in range(1, NX):
        arrived(gb.at[e], agc, (e, 0))
    for s in range(HA, G):
        v = jnp.stack([gb[e, :, s - HA] for e in range(NX)], axis=1)
        lhs[:, s * BLOCK:(s + 1) * BLOCK] = v.reshape(sz.C, BLOCK)
    prod = lax.dot_general(lhs[...], coup_v[...], (((1,), (1,)), ((), ())), preferred_element_type=F32)
    for t in range(NY):
        ycs[t] = sz.pack(prod[t * sz.CY:(t + 1) * sz.CY, :])
    for d in far_first(NY):
        y1s[d] = ycs[yd(d)].astype(BF)
        send(y1s.at[d], ycr.at[d], y1sem, (d,), dev_y(d))

    def first_block(zz):
        return (sz.TZ * zz) // BLOCK

    for d in far_first(NZ):
        send(sol.at[pl.ds(first_block(zd(d)), sz.SPAN)], o1.at[z], o1sem, (d,), dev_z(d))
    o1[z] = sol[pl.ds(first_block(z), sz.SPAN)]

    load_crhs.wait()
    crhs_t[...] = crhs_v[...].astype(F32).T
    load_cinv.wait()
    for j in range(sz.T3 // BLOCK):
        cols = slice(j * BLOCK, (j + 1) * BLOCK)
        cit[cols, :] = cinv_v[:, cols].astype(F32).T.astype(BF)

    acc = ycs[r]
    for d in far_first(NY)[::-1]:
        arrived(ycr.at[d], y1sem, (d,))
        acc = acc + ycr[d].astype(F32)
    acc = sz.unpack(acc)
    from_z = zd(-near(r))
    diff = []
    for e in range(NX):
        rows = pl.ds(pl.multiple_of((from_z * NX + xd(-e)) * 8, 8), 8)
        diff.append(crhs_t[rows, :] - acc[e * 8:(e + 1) * 8, :])
    red[0] = sz.pack(jnp.concatenate(diff, axis=0)).astype(BF)
    for d in far_first(NY):
        send(red.at[0], red.at[d], y2sem, (d,), dev_y(d))

    for d in range(1, NZ):
        arrived(o1.at[zd(-d)], o1sem, (d,))
    for d in range(1, NX):
        send(o1, o2.at[x], o2sem, (d,), dev_x(d))
    o2[x] = o1[...]
    drain()
    for d in range(1, NX):
        arrived(o2.at[xd(-d)], o2sem, (d,))
    for b in range(sz.SPAN):
        v = jnp.stack([o2[e, :, b] for e in range(NX)], axis=1)
        ot[b * BLOCK:(b + 1) * BLOCK, :] = v.astype(F32).reshape(sz.C, BLOCK).T
    first_row = sz.TZ * z + (2 * x + k) * sz.TO - first_block(z) * BLOCK
    out[:sz.TO] = ot[pl.ds(pl.multiple_of(first_row, 8), sz.TO), :].astype(BF)

    for d in range(1, NY):
        arrived(red.at[d], y2sem, (d,))
    for d in range(NY):
        v = sz.unpack(red[d].astype(F32)).astype(BF).reshape(NX, 8, sz.S3)
        for e in range(NX):
            red_s[zd(-near(yd(-d))), xd(-e)] = v[e]
    reduced = red_s[...].reshape(sz.C, sz.S3)
    rows_z = NX * sz.TC
    for d in order:
        rows = pl.ds(pl.multiple_of(zd(d) * rows_z, rows_z), rows_z)
        v = lax.dot_general(cit[rows, :], reduced, (((1,), (1,)), ((), ())), preferred_element_type=F32)
        p5f[d] = v.reshape(NX, sz.TC, sz.C)
        if d:
            w5s[d] = p5f[d, :, RA:].astype(BF)
            send(w5s.at[d], w5r.at[d], w5sem, (d,), dev_z(d), to=(0,))
        for e in far_first(NX):
            p5s[d, e] = p5f[d, xd(e), :RA].astype(BF)
            send(p5s.at[d, e], p5r.at[d, e], p5sem, (d, e), dev_x(e), to=(d, 0))
    for d in order:
        acc = p5f[d, x, :RA]
        arrived(p5r.at[d, pl.ds(1, NX - 1)], p5sem, (d, 0))
        for e in range(1, NX):
            acc = acc + p5r[d, e].astype(F32)
        if d:
            z5s[d] = acc.astype(BF)
            send(z5s.at[d], z5r.at[d], z5sem, (d,), dev_z(d))
    p5f[0, x, :RA] = acc
    acc = p5f[0, :, RA:]
    arrived(w5r.at[pl.ds(1, NZ - 1)], w5sem, (0,))
    for d in range(1, NZ):
        acc = acc + w5r[d].astype(F32)
    p5f[0, :, RA:] = acc
    for e in far_first(NX):
        t5s[e] = p5f[0, xd(e), RA:].astype(BF)
        send(t5s.at[e], t5r.at[e], t5sem, (e,), dev_x(e), to=(0,))
    drain()
    acc = p5f[0, x, :RA]
    for d in far_first(NZ):
        arrived(z5r.at[d], z5sem, (d,))
        acc = acc + z5r[d].astype(F32)
    out[sz.TO:sz.TO + RA] = acc.astype(BF)
    acc = p5f[0, x, RA:]
    arrived(t5r.at[pl.ds(1, NX - 1)], t5sem, (0,))
    for e in range(1, NX):
        acc = acc + t5r[e].astype(F32)
    out[sz.TO + RA:] = acc.astype(BF)


def per_device(mesh, root_rhs, root_inverse, child_rhs, child_inverse, coupling, block_map, block_count):
    sz = Sizes(mesh, root_rhs, root_inverse, child_inverse, coupling)
    coupling = jnp.swapaxes(coupling, 1, 2)
    NX, NZ, NY, HB, Q, G, HA = sz.NX, sz.NZ, sz.NY, sz.HB, sz.Q, sz.G, sz.HA
    AB, RA = sz.AB, sz.RA
    vmem = pl.BlockSpec(memory_space=pltpu.VMEM)
    hbm = pl.BlockSpec(memory_space=pl.ANY)

    def dma(*shape):
        return pltpu.SemaphoreType.DMA((2,) + shape)

    scratch = dict(
        rrhs_v=pltpu.VMEM((sz.S1, sz.C), BF),
        rinv_v=pltpu.VMEM((sz.S1, sz.T1), BF),
        crhs_v=pltpu.VMEM((sz.S3, sz.C), BF),
        coup_v=pltpu.VMEM((sz.S3, sz.U), BF),
        cinv_v=pltpu.VMEM((sz.S3, sz.T3), BF),
        bmap_s=pltpu.SMEM(block_map.shape, jnp.int32),
        bcnt_s=pltpu.SMEM(block_count.shape, jnp.int32),
        cit=pltpu.VMEM((sz.T3, sz.S3), BF),
        rhs_t=pltpu.VMEM((sz.C, sz.S1), BF),
        crhs_t=pltpu.VMEM((sz.C, sz.S3), F32),
        cs=pltpu.VMEM((NZ, NX, HB, 8, BLOCK), F32),
        cr=pltpu.VMEM((NZ, NX, HB, 8, BLOCK), F32),
        own=pltpu.VMEM((NZ, NX, HB, 8, BLOCK), F32),
        xs=pltpu.VMEM((NZ, NX, AB, 8, BLOCK), BF),
        xr=pltpu.VMEM((NZ, NX, AB, 8, BLOCK), BF),
        zs=pltpu.VMEM((NZ, AB, 8, BLOCK), BF),
        zr=pltpu.VMEM((NZ, AB, 8, BLOCK), BF),
        ws=pltpu.VMEM((NZ, NX, HB - AB, 8, BLOCK), BF),
        wr=pltpu.VMEM((NZ, NX, HB - AB, 8, BLOCK), BF),
        ts=pltpu.VMEM((NX, HB - AB, 8, BLOCK), BF),
        tr=pltpu.VMEM((NX, HB - AB, 8, BLOCK), BF),
        sol=pltpu.VMEM((sz.NB, 8, BLOCK), BF),
        ysd=pltpu.VMEM((NY, CAP, 8, BLOCK), BF),
        yrc=pltpu.VMEM((NY * CAP, 8, BLOCK), BF),
        ga=pltpu.VMEM((NZ, NX, HA, 8, BLOCK), BF),
        gb=pltpu.VMEM((NX, NZ, G - HA, 8, BLOCK), BF),
        lhs=pltpu.VMEM((sz.C, sz.U), BF),
        ycs=pltpu.VMEM((NY,) + sz.packed, F32),
        y1s=pltpu.VMEM((NY,) + sz.packed, BF),
        ycr=pltpu.VMEM((NY,) + sz.packed, BF),
        red=pltpu.VMEM((NY,) + sz.packed, BF),
        red_s=pltpu.VMEM((NZ, NX, 8, sz.S3), BF),
        o1=pltpu.VMEM((NZ, sz.SPAN, 8, BLOCK), BF),
        o2=pltpu.VMEM((NX, NZ, sz.SPAN, 8, BLOCK), BF),
        ot=pltpu.VMEM((sz.SPAN * BLOCK, sz.C), F32),
        p5f=pltpu.VMEM((NZ, NX, sz.TC, sz.C), F32),
        p5s=pltpu.VMEM((NZ, NX, RA, sz.C), BF),
        p5r=pltpu.VMEM((NZ, NX, RA, sz.C), BF),
        z5s=pltpu.VMEM((NZ, RA, sz.C), BF),
        z5r=pltpu.VMEM((NZ, RA, sz.C), BF),
        w5s=pltpu.VMEM((NZ, NX, sz.TC - RA, sz.C), BF),
        w5r=pltpu.VMEM((NZ, NX, sz.TC - RA, sz.C), BF),
        t5s=pltpu.VMEM((NX, sz.TC - RA, sz.C), BF),
        t5r=pltpu.VMEM((NX, sz.TC - RA, sz.C), BF),
        sel=pltpu.SMEM((NY * CAP,), jnp.int32),
        pos=pltpu.SMEM((G,), jnp.int32),
        lsem=pltpu.SemaphoreType.DMA((8,)),
        csem=dma(NZ),
        xsem=dma(NZ, NX),
        zsem=dma(NZ),
        wsem=dma(NZ),
        tsem=dma(NX),
        c2sem=dma(1),
        ysem=dma(NY),
        o1sem=dma(NZ),
        o2sem=dma(NX),
        agx=dma(NX),
        aga=dma(NZ),
        agz=dma(NZ),
        agc=dma(NX, NZ),
        y1sem=dma(NY),
        y2sem=dma(NY),
        p5sem=dma(NZ, NX),
        z5sem=dma(NZ),
        w5sem=dma(NZ),
        t5sem=dma(NX),
    )
    names = list(scratch)

    def body(*refs):
        kernel(sz, *refs[:8], **dict(zip(names, refs[8:])))

    both = pl.pallas_call(
        body,
        name="backward",
        out_shape=pltpu.VMEM((sz.TO + sz.TC, sz.C), BF),
        in_specs=[hbm] * 7,
        out_specs=vmem,
        scratch_shapes=list(scratch.values()),
        compiler_params=pltpu.CompilerParams(
            collective_id=0, has_side_effects=True, vmem_limit_bytes=56 * 1024 * 1024
        ),
    )(root_rhs, root_inverse, child_rhs, child_inverse, coupling, block_map, block_count)
    return both[:sz.TO], both[sz.TO:][None]


def solution(mesh):
    in_specs = (
        P(("col", "cores"), None),
        P(("col", "cores"), "row"),
        P("cores", "col", None),
        P("cores", "col", "row"),
        P("cores", "row", "col"),
        P(),
        P(),
    )
    out_specs = (P(("row", "col", "cores"), None), P("cores", ("row", "col"), None))
    return jax.shard_map(
        functools.partial(per_device, mesh),
        mesh=mesh, in_specs=in_specs, out_specs=out_specs, check_vma=False,
    )
```

```python
import functools

import jax
import jax.numpy as jnp
from jax import lax
from jax.experimental import pallas as pl
from jax.experimental.pallas import tpu as pltpu
from jax.sharding import PartitionSpec as P

BLOCK = 128
CAP = 3
GRID = {32: (4, 8), 4: (2, 2)}
MESH = pl.DeviceIdType.MESH
BF = jnp.bfloat16
F32 = jnp.float32


class Sizes:
    def __init__(self, mesh, root_rhs, root_inverse, child_inverse, coupling):
        self.NY = mesh.shape["row"]
        self.NX, self.NZ = GRID[mesh.shape["col"]]
        self.Q = self.NX * self.NZ
        self.S1, self.C = root_rhs.shape
        self.T1 = root_inverse.shape[1]
        self.NB = self.T1 // BLOCK
        self.HB = self.NB // 2
        self.S3, self.T3 = child_inverse.shape[1:]
        self.U = coupling.shape[1]
        self.G = self.U // BLOCK
        self.HA = max(self.G // 5, 1)
        self.SY = self.S3 // self.NY
        self.TO = self.T1 // (2 * self.Q)
        self.TC = self.T3 // self.Q
        self.TZ = self.T1 // self.NZ
        self.AB = max(8 * self.HB // 10, 1)
        self.RA = self.TC - 8
        starts = [self.TZ * z // BLOCK for z in range(self.NZ)]
        ends = [-(-self.TZ * (z + 1) // BLOCK) for z in range(self.NZ)]
        self.SPAN = max(e - s for s, e in zip(starts, ends))


def far_first(n):
    return sorted(range(1, n), key=lambda d: (-min(d, n - d), d))


def kernel(
    sz, rrhs, rinv, crhs, cinv, coup, bmap, bcnt, out, *,
    rrhs_v, rinv_v, crhs_v, coup_v, cinv_v, bmap_s, bcnt_s, cit, rhs_t, crhs_f, cs, cr, own, xs, xr, zs, zr, ws, wr, ts, tr, sol,
    ysd, yrc, ga, gb, lhs, ycs, y1s, ycr, red, o1, o2, ot, p5f, p5s, p5r, z5s, z5r, w5s, w5r, t5s, t5r, sel, pos,
    lsem, csem, xsem, zsem, wsem, tsem, c2sem, ysem, o1sem, o2sem, agx, aga, agz, agc, y1sem, y2sem, p5sem, z5sem, w5sem, t5sem,
):
    NX, NZ, NY, HB, NB, G, HA = sz.NX, sz.NZ, sz.NY, sz.HB, sz.NB, sz.G, sz.HA
    r, c, k = lax.axis_index("row"), lax.axis_index("col"), lax.axis_index("cores")
    z, x = c // NX, lax.rem(c, NX)
    AB, RA = sz.AB, sz.RA

    def xd(d):
        return lax.rem(x + d + NX, NX)

    def zd(d):
        return lax.rem(z + d + NZ, NZ)

    def yd(d):
        return lax.rem(r + d + NY, NY)

    def dev_x(d):
        return (r, z * NX + xd(d), k)

    def dev_z(d):
        return (r, zd(d) * NX + x, k)

    def dev_y(d):
        return (yd(d), c, k)

    def near(i):
        if isinstance(i, int):
            return NZ - (i + 1) // 2 if i % 2 else i // 2
        return jnp.where(lax.rem(i, 2) == 1, NZ - (i + 1) // 2, i // 2)

    dev_c = (r, c, 1 - k)
    sent = []

    def send(src, dst, sem, idx, dev, to=None):
        cp = pltpu.make_async_remote_copy(
            src_ref=src, dst_ref=dst, send_sem=sem.at[(0,) + idx], recv_sem=sem.at[(1,) + (to or idx)],
            device_id=dev, device_id_type=MESH,
        )
        cp.start()
        sent.append(cp)

    def drain():
        for cp in sent:
            cp.wait_send()
        sent.clear()

    def arrived(ref, sem, idx):
        pltpu.make_async_remote_copy(
            src_ref=ref, dst_ref=ref, send_sem=sem.at[(0,) + idx], recv_sem=sem.at[(1,) + idx],
            device_id=dev_c, device_id_type=MESH,
        ).wait_recv()

    half = HB * BLOCK
    theirs = pl.ds(pl.multiple_of((1 - k) * half, BLOCK), half)
    ours = pl.ds(pl.multiple_of(k * half, BLOCK), half)
    pairs = [
        (rrhs, rrhs_v), (rinv.at[:, theirs], rinv_v.at[:, theirs]), (rinv.at[:, ours], rinv_v.at[:, ours]),
        (bmap, bmap_s), (bcnt, bcnt_s), (cinv.at[0], cinv_v), (crhs.at[0], crhs_v), (coup.at[0], coup_v),
    ]
    loads = [pltpu.make_async_copy(a, b, lsem.at[i]) for i, (a, b) in enumerate(pairs)]
    for cp in loads[:3]:
        cp.start()
    load_rrhs, load_theirs, load_ours, load_map, load_count, load_cinv, load_crhs, load_coup = loads

    barrier = pltpu.get_barrier_semaphore()
    peers = (
        [dev_c]
        + [dev_x(d) for d in range(1, NX)]
        + [dev_z(d) for d in range(1, NZ)]
        + [dev_y(d) for d in range(1, NY)]
    )
    for dev in peers:
        pl.semaphore_signal(barrier, inc=1, device_id=dev, device_id_type=MESH)

    def partial(which, dst):
        for b in range(0, HB, 2):
            off = pl.multiple_of(which * half + b * BLOCK, BLOCK)
            v = jnp.dot(rhs_t[...], rinv_v[:, pl.ds(off, 2 * BLOCK)], preferred_element_type=F32)
            for i in range(2):
                dst[:, :, b + i] = v[:, i * BLOCK:(i + 1) * BLOCK].reshape(NZ, NX, 8, BLOCK)

    order = far_first(NZ) + [0]
    load_rrhs.wait()
    rhs_t[...] = rrhs_v[...].astype(F32).T.astype(BF)
    load_theirs.wait()
    partial(1 - k, cs)
    load_ours.wait()
    partial(k, own)
    for cp in loads[3:]:
        cp.start()
    pl.semaphore_wait(barrier, len(peers))
    for d in order:
        send(cs.at[zd(d)], cr.at[zd(d)], csem, (d,), dev_c)

    for d in order:
        arrived(cr.at[zd(d)], csem, (d,))
        if d:
            ws[d] = (own[zd(d), :, AB:] + cr[zd(d), :, AB:]).astype(BF)
            send(ws.at[d], wr.at[d], wsem, (d,), dev_z(d), to=(0,))
        for e in far_first(NX):
            xs[d, e] = (own[zd(d), xd(e), :AB] + cr[zd(d), xd(e), :AB]).astype(BF)
            send(xs.at[d, e], xr.at[d, e], xsem, (d, e), dev_x(e), to=(d, 0))
    for d in order:
        acc = own[zd(d), x, :AB] + cr[zd(d), x, :AB]
        arrived(xr.at[d, pl.ds(1, NX - 1)], xsem, (d, 0))
        for e in range(1, NX):
            acc = acc + xr[d, e].astype(F32)
        if d:
            zs[d] = acc.astype(BF)
            send(zs.at[d], zr.at[d], zsem, (d,), dev_z(d))
        else:
            own[z, x, :AB] = acc
    acc = own[z, :, AB:] + cr[z, :, AB:]
    arrived(wr.at[pl.ds(1, NZ - 1)], wsem, (0,))
    for d in range(1, NZ):
        acc = acc + wr[d].astype(F32)
    own[z, :, AB:] = acc
    for e in far_first(NX):
        ts[e] = own[z, xd(e), AB:].astype(BF)
        send(ts.at[e], tr.at[e], tsem, (e,), dev_x(e), to=(0,))

    def choose(t, _):
        cnt = jnp.int32(0)
        got = [jnp.int32(0)] * CAP
        for s in range(G):
            b = bmap_s[k, t * G + s] - r * NB
            inside = jnp.logical_and(b >= 0, b < NB)
            for j in range(CAP):
                got[j] = jnp.where(jnp.logical_and(inside, cnt == j), b, got[j])
            cnt = cnt + jnp.where(inside, 1, 0)
        for j in range(CAP):
            sel[t * CAP + j] = got[j]
        return 0

    load_map.wait()
    load_count.wait()
    lax.fori_loop(0, NY, choose, 0)

    acc = own[z, x, :AB]
    for d in far_first(NZ):
        arrived(zr.at[d], zsem, (d,))
        acc = acc + zr[d].astype(F32)
    sol[pl.ds(k * HB, AB)] = acc.astype(BF)
    acc = own[z, x, AB:]
    arrived(tr.at[pl.ds(1, NX - 1)], tsem, (0,))
    for e in range(1, NX):
        acc = acc + tr[e].astype(F32)
    sol[pl.ds(k * HB + AB, HB - AB)] = acc.astype(BF)
    mine = pl.ds(k * HB, HB)
    send(sol.at[mine], sol.at[mine], c2sem, (0,), dev_c)
    arrived(sol.at[pl.ds((1 - k) * HB, HB)], c2sem, (0,))

    for d in far_first(NY) + [0]:
        t = yd(d)
        for j in range(CAP):
            v = sol[sel[t * CAP + j]]
            if d:
                ysd[d, j] = v
            else:
                yrc[r * CAP + j] = v
        if d:
            send(ysd.at[d], yrc.at[pl.ds(r * CAP, CAP)], ysem, (d,), dev_y(d))

    ranges = [lax.div(bmap_s[k, r * G + s], jnp.int32(NB)) for s in range(G)]
    for s in range(G):
        rank = jnp.int32(0)
        for e in range(s):
            rank = rank + jnp.where(ranges[e] == ranges[s], 1, 0)
        pos[s] = ranges[s] * CAP + jnp.minimum(rank, CAP - 1)
    drain()
    for d in range(1, NY):
        arrived(yrc.at[pl.ds(yd(-d) * CAP, CAP)], ysem, (d,))
    for s in [*range(HA, G), *range(HA)]:
        v = yrc[pos[s]]
        alive = r * G + s < bcnt_s[k]
        v = jnp.where(alive, v.astype(F32), 0.0).astype(BF)
        if s < HA:
            ga[0, 0, s] = v
        else:
            gb[0, 0, s - HA] = v

    for e in far_first(NX):
        send(ga.at[0, 0], ga.at[0, e], agx, (e,), dev_x(e))
    for i in range(1, NZ):
        send(gb.at[0, 0], gb.at[0, i], agz, (i,), dev_z(near(i)))

    def spread(i):
        for e in range(1, NX):
            send(gb.at[0, i], gb.at[e, i], agc, (e, i), dev_x(e), to=(e, 0))

    spread(0)
    for e in range(1, NX):
        arrived(ga.at[0, e], agx, (e,))
    for i in range(1, NZ):
        send(ga.at[0], ga.at[i], aga, (i,), dev_z(near(i)))
    for i in range(1, NZ):
        arrived(gb.at[0, i], agz, (i,))
        spread(i)
    load_coup.wait()

    def place(i, e):
        q = zd(-near(i)) * NX + xd(-e)
        for s in range(G):
            lhs[q, :, s * BLOCK:(s + 1) * BLOCK] = ga[i, e, s] if s < HA else gb[e, i, s - HA]

    for i in range(1, NZ):
        arrived(ga.at[i], aga, (i,))
    for e in range(NX):
        if e:
            arrived(gb.at[e], agc, (e, 0))
        for i in range(NZ):
            place(i, e)
    prod = lax.dot_general(
        coup_v[...], lhs[...].reshape(sz.C, sz.U), (((1,), (1,)), ((), ())), preferred_element_type=F32)
    ycs[...] = prod.reshape(NY, sz.SY, sz.C)
    for d in far_first(NY):
        y1s[d] = ycs[yd(d)].astype(BF)
        send(y1s.at[d], ycr.at[d], y1sem, (d,), dev_y(d))

    def first_block(zz):
        return (sz.TZ * zz) // BLOCK

    for d in far_first(NZ):
        send(sol.at[pl.ds(first_block(zd(d)), sz.SPAN)], o1.at[z], o1sem, (d,), dev_z(d))
    o1[z] = sol[pl.ds(first_block(z), sz.SPAN)]

    load_crhs.wait()
    crhs_f[...] = crhs_v[...].astype(F32).reshape(NY, sz.SY, sz.C)
    load_cinv.wait()
    for j in range(sz.T3 // BLOCK):
        cols = slice(j * BLOCK, (j + 1) * BLOCK)
        cit[cols, :] = cinv_v[:, cols].astype(F32).T.astype(BF)

    acc = ycs[r]
    for d in far_first(NY)[::-1]:
        arrived(ycr.at[d], y1sem, (d,))
        acc = acc + ycr[d].astype(F32)
    red[r] = (crhs_f[r] - acc).astype(BF)
    for d in far_first(NY):
        send(red.at[r], red.at[r], y2sem, (d,), dev_y(d))

    for d in range(1, NZ):
        arrived(o1.at[zd(-d)], o1sem, (d,))
    for d in range(1, NX):
        send(o1, o2.at[x], o2sem, (d,), dev_x(d))
    o2[x] = o1[...]
    drain()
    for d in range(1, NX):
        arrived(o2.at[xd(-d)], o2sem, (d,))
    for b in range(sz.SPAN):
        v = jnp.stack([o2[e, :, b] for e in range(NX)], axis=1)
        ot[b * BLOCK:(b + 1) * BLOCK, :] = v.astype(F32).reshape(sz.C, BLOCK).T
    first_row = sz.TZ * z + (2 * x + k) * sz.TO - first_block(z) * BLOCK
    out[:sz.TO] = ot[pl.ds(pl.multiple_of(first_row, 8), sz.TO), :].astype(BF)

    for d in range(1, NY):
        arrived(red.at[yd(-d)], y2sem, (d,))
    reduced = red[...].astype(F32).reshape(sz.S3, sz.C).astype(BF)
    rows_z = NX * sz.TC
    for d in order:
        rows = pl.ds(pl.multiple_of(zd(d) * rows_z, rows_z), rows_z)
        v = jnp.dot(cit[rows, :], reduced, preferred_element_type=F32)
        p5f[d] = v.reshape(NX, sz.TC, sz.C)
        if d:
            w5s[d] = p5f[d, :, RA:].astype(BF)
            send(w5s.at[d], w5r.at[d], w5sem, (d,), dev_z(d), to=(0,))
        for e in far_first(NX):
            p5s[d, e] = p5f[d, xd(e), :RA].astype(BF)
            send(p5s.at[d, e], p5r.at[d, e], p5sem, (d, e), dev_x(e), to=(d, 0))
    for d in order:
        acc = p5f[d, x, :RA]
        arrived(p5r.at[d, pl.ds(1, NX - 1)], p5sem, (d, 0))
        for e in range(1, NX):
            acc = acc + p5r[d, e].astype(F32)
        if d:
            z5s[d] = acc.astype(BF)
            send(z5s.at[d], z5r.at[d], z5sem, (d,), dev_z(d))
    p5f[0, x, :RA] = acc
    acc = p5f[0, :, RA:]
    arrived(w5r.at[pl.ds(1, NZ - 1)], w5sem, (0,))
    for d in range(1, NZ):
        acc = acc + w5r[d].astype(F32)
    p5f[0, :, RA:] = acc
    for e in far_first(NX):
        t5s[e] = p5f[0, xd(e), RA:].astype(BF)
        send(t5s.at[e], t5r.at[e], t5sem, (e,), dev_x(e), to=(0,))
    drain()
    acc = p5f[0, x, :RA]
    for d in far_first(NZ):
        arrived(z5r.at[d], z5sem, (d,))
        acc = acc + z5r[d].astype(F32)
    out[sz.TO:sz.TO + RA] = acc.astype(BF)
    acc = p5f[0, x, RA:]
    arrived(t5r.at[pl.ds(1, NX - 1)], t5sem, (0,))
    for e in range(1, NX):
        acc = acc + t5r[e].astype(F32)
    out[sz.TO + RA:] = acc.astype(BF)


def per_device(mesh, root_rhs, root_inverse, child_rhs, child_inverse, coupling, block_map, block_count):
    sz = Sizes(mesh, root_rhs, root_inverse, child_inverse, coupling)
    coupling = jnp.swapaxes(coupling, 1, 2)
    NX, NZ, NY, HB, Q, G, HA = sz.NX, sz.NZ, sz.NY, sz.HB, sz.Q, sz.G, sz.HA
    AB, RA = sz.AB, sz.RA
    vmem = pl.BlockSpec(memory_space=pltpu.VMEM)
    hbm = pl.BlockSpec(memory_space=pl.ANY)

    def dma(*shape):
        return pltpu.SemaphoreType.DMA((2,) + shape)

    scratch = dict(
        rrhs_v=pltpu.VMEM((sz.S1, sz.C), BF),
        rinv_v=pltpu.VMEM((sz.S1, sz.T1), BF),
        crhs_v=pltpu.VMEM((sz.S3, sz.C), BF),
        coup_v=pltpu.VMEM((sz.S3, sz.U), BF),
        cinv_v=pltpu.VMEM((sz.S3, sz.T3), BF),
        bmap_s=pltpu.SMEM(block_map.shape, jnp.int32),
        bcnt_s=pltpu.SMEM(block_count.shape, jnp.int32),
        cit=pltpu.VMEM((sz.T3, sz.S3), BF),
        rhs_t=pltpu.VMEM((sz.C, sz.S1), BF),
        crhs_f=pltpu.VMEM((NY, sz.SY, sz.C), F32),
        cs=pltpu.VMEM((NZ, NX, HB, 8, BLOCK), F32),
        cr=pltpu.VMEM((NZ, NX, HB, 8, BLOCK), F32),
        own=pltpu.VMEM((NZ, NX, HB, 8, BLOCK), F32),
        xs=pltpu.VMEM((NZ, NX, AB, 8, BLOCK), BF),
        xr=pltpu.VMEM((NZ, NX, AB, 8, BLOCK), BF),
        zs=pltpu.VMEM((NZ, AB, 8, BLOCK), BF),
        zr=pltpu.VMEM((NZ, AB, 8, BLOCK), BF),
        ws=pltpu.VMEM((NZ, NX, HB - AB, 8, BLOCK), BF),
        wr=pltpu.VMEM((NZ, NX, HB - AB, 8, BLOCK), BF),
        ts=pltpu.VMEM((NX, HB - AB, 8, BLOCK), BF),
        tr=pltpu.VMEM((NX, HB - AB, 8, BLOCK), BF),
        sol=pltpu.VMEM((sz.NB, 8, BLOCK), BF),
        ysd=pltpu.VMEM((NY, CAP, 8, BLOCK), BF),
        yrc=pltpu.VMEM((NY * CAP, 8, BLOCK), BF),
        ga=pltpu.VMEM((NZ, NX, HA, 8, BLOCK), BF),
        gb=pltpu.VMEM((NX, NZ, G - HA, 8, BLOCK), BF),
        lhs=pltpu.VMEM((Q, 8, sz.U), BF),
        ycs=pltpu.VMEM((NY, sz.SY, sz.C), F32),
        y1s=pltpu.VMEM((NY, sz.SY, sz.C), BF),
        ycr=pltpu.VMEM((NY, sz.SY, sz.C), BF),
        red=pltpu.VMEM((NY, sz.SY, sz.C), BF),
        o1=pltpu.VMEM((NZ, sz.SPAN, 8, BLOCK), BF),
        o2=pltpu.VMEM((NX, NZ, sz.SPAN, 8, BLOCK), BF),
        ot=pltpu.VMEM((sz.SPAN * BLOCK, sz.C), F32),
        p5f=pltpu.VMEM((NZ, NX, sz.TC, sz.C), F32),
        p5s=pltpu.VMEM((NZ, NX, RA, sz.C), BF),
        p5r=pltpu.VMEM((NZ, NX, RA, sz.C), BF),
        z5s=pltpu.VMEM((NZ, RA, sz.C), BF),
        z5r=pltpu.VMEM((NZ, RA, sz.C), BF),
        w5s=pltpu.VMEM((NZ, NX, sz.TC - RA, sz.C), BF),
        w5r=pltpu.VMEM((NZ, NX, sz.TC - RA, sz.C), BF),
        t5s=pltpu.VMEM((NX, sz.TC - RA, sz.C), BF),
        t5r=pltpu.VMEM((NX, sz.TC - RA, sz.C), BF),
        sel=pltpu.SMEM((NY * CAP,), jnp.int32),
        pos=pltpu.SMEM((G,), jnp.int32),
        lsem=pltpu.SemaphoreType.DMA((8,)),
        csem=dma(NZ),
        xsem=dma(NZ, NX),
        zsem=dma(NZ),
        wsem=dma(NZ),
        tsem=dma(NX),
        c2sem=dma(1),
        ysem=dma(NY),
        o1sem=dma(NZ),
        o2sem=dma(NX),
        agx=dma(NX),
        aga=dma(NZ),
        agz=dma(NZ),
        agc=dma(NX, NZ),
        y1sem=dma(NY),
        y2sem=dma(NY),
        p5sem=dma(NZ, NX),
        z5sem=dma(NZ),
        w5sem=dma(NZ),
        t5sem=dma(NX),
    )
    names = list(scratch)

    def body(*refs):
        kernel(sz, *refs[:8], **dict(zip(names, refs[8:])))

    both = pl.pallas_call(
        body,
        name="backward",
        out_shape=pltpu.VMEM((sz.TO + sz.TC, sz.C), BF),
        in_specs=[hbm] * 7,
        out_specs=vmem,
        scratch_shapes=list(scratch.values()),
        compiler_params=pltpu.CompilerParams(
            collective_id=0, has_side_effects=True, vmem_limit_bytes=56 * 1024 * 1024
        ),
    )(root_rhs, root_inverse, child_rhs, child_inverse, coupling, block_map, block_count)
    return both[:sz.TO], both[sz.TO:][None]


def solution(mesh):
    in_specs = (
        P(("col", "cores"), None),
        P(("col", "cores"), "row"),
        P("cores", "col", None),
        P("cores", "col", "row"),
        P("cores", "row", "col"),
        P(),
        P(),
    )
    out_specs = (P(("row", "col", "cores"), None), P("cores", ("row", "col"), None))
    return jax.shard_map(
        functools.partial(per_device, mesh),
        mesh=mesh, in_specs=in_specs, out_specs=out_specs, check_vma=False,
    )
```

```python
import functools

import jax
import jax.numpy as jnp
from jax import lax
from jax.experimental import pallas as pl
from jax.experimental.pallas import tpu as pltpu
from jax.sharding import PartitionSpec as P

BLOCK = 128
CAP = 3
GRID = {32: (4, 8), 4: (2, 2)}
MESH = pl.DeviceIdType.MESH
BF = jnp.bfloat16
F32 = jnp.float32


class Sizes:
    def __init__(self, mesh, root_rhs, root_inverse, child_inverse, coupling):
        self.NY = mesh.shape["row"]
        self.NX, self.NZ = GRID[mesh.shape["col"]]
        self.Q = self.NX * self.NZ
        self.S1, self.C = root_rhs.shape
        self.T1 = root_inverse.shape[1]
        self.NB = self.T1 // BLOCK
        self.HB = self.NB // 2
        self.S3, self.T3 = child_inverse.shape[1:]
        self.U = coupling.shape[1]
        self.G = self.U // BLOCK
        self.HA = max(self.G // 5, 1)
        self.SY = self.S3 // self.NY
        self.TO = self.T1 // (2 * self.Q)
        self.TC = self.T3 // self.Q
        self.TZ = self.T1 // self.NZ
        self.AB = max(8 * self.HB // 10, 1)
        self.RA = self.TC - 8
        starts = [self.TZ * z // BLOCK for z in range(self.NZ)]
        ends = [-(-self.TZ * (z + 1) // BLOCK) for z in range(self.NZ)]
        self.SPAN = max(e - s for s, e in zip(starts, ends))


def far_first(n):
    return sorted(range(1, n), key=lambda d: (-min(d, n - d), d))


def kernel(
    sz, rrhs, rinv, crhs, cinv, coup, bmap, bcnt, out, *,
    rrhs_v, rinv_v, crhs_v, coup_v, cinv_v, bmap_s, bcnt_s, cit, rhs_t, crhs_f, cs, cr, own, xs, xr, zs, zr, ws, wr, ts, tr, sol,
    ysd, yrc, ga, gb, lhs, ycs, y1s, ycr, red, o1, o2, ot, p5f, p5s, p5r, z5s, z5r, w5s, w5r, t5s, t5r, sel, pos,
    lsem, csem, xsem, zsem, wsem, tsem, c2sem, ysem, o1sem, o2sem, agx, aga, agz, agc, y1sem, y2sem, p5sem, z5sem, w5sem, t5sem,
):
    NX, NZ, NY, HB, NB, G, HA = sz.NX, sz.NZ, sz.NY, sz.HB, sz.NB, sz.G, sz.HA
    r, c, k = lax.axis_index("row"), lax.axis_index("col"), lax.axis_index("cores")
    z, x = c // NX, lax.rem(c, NX)
    AB, RA = sz.AB, sz.RA

    def xd(d):
        return lax.rem(x + d + NX, NX)

    def zd(d):
        return lax.rem(z + d + NZ, NZ)

    def yd(d):
        return lax.rem(r + d + NY, NY)

    def dev_x(d):
        return (r, z * NX + xd(d), k)

    def dev_z(d):
        return (r, zd(d) * NX + x, k)

    def dev_y(d):
        return (yd(d), c, k)

    def near(i):
        if isinstance(i, int):
            return NZ - (i + 1) // 2 if i % 2 else i // 2
        return jnp.where(lax.rem(i, 2) == 1, NZ - (i + 1) // 2, i // 2)

    dev_c = (r, c, 1 - k)
    sent = []

    def send(src, dst, sem, idx, dev, to=None):
        cp = pltpu.make_async_remote_copy(
            src_ref=src, dst_ref=dst, send_sem=sem.at[(0,) + idx], recv_sem=sem.at[(1,) + (to or idx)],
            device_id=dev, device_id_type=MESH,
        )
        cp.start()
        sent.append(cp)

    def drain():
        for cp in sent:
            cp.wait_send()
        sent.clear()

    def arrived(ref, sem, idx):
        pltpu.make_async_remote_copy(
            src_ref=ref, dst_ref=ref, send_sem=sem.at[(0,) + idx], recv_sem=sem.at[(1,) + idx],
            device_id=dev_c, device_id_type=MESH,
        ).wait_recv()

    half = HB * BLOCK
    theirs = pl.ds(pl.multiple_of((1 - k) * half, BLOCK), half)
    ours = pl.ds(pl.multiple_of(k * half, BLOCK), half)
    pairs = [
        (rrhs, rrhs_v), (rinv.at[:, theirs], rinv_v.at[:, theirs]), (rinv.at[:, ours], rinv_v.at[:, ours]),
        (bmap, bmap_s), (bcnt, bcnt_s), (cinv.at[0], cinv_v), (crhs.at[0], crhs_v), (coup.at[0], coup_v),
    ]
    loads = [pltpu.make_async_copy(a, b, lsem.at[i]) for i, (a, b) in enumerate(pairs)]
    for cp in loads[:3]:
        cp.start()
    load_rrhs, load_theirs, load_ours, load_map, load_count, load_cinv, load_crhs, load_coup = loads

    barrier = pltpu.get_barrier_semaphore()
    peers = (
        [dev_c]
        + [dev_x(d) for d in range(1, NX)]
        + [dev_z(d) for d in range(1, NZ)]
        + [dev_y(d) for d in range(1, NY)]
    )
    for dev in peers:
        pl.semaphore_signal(barrier, inc=1, device_id=dev, device_id_type=MESH)

    def partial(which, dst):
        for b in range(0, HB, 2):
            off = pl.multiple_of(which * half + b * BLOCK, BLOCK)
            v = jnp.dot(rhs_t[...], rinv_v[:, pl.ds(off, 2 * BLOCK)], preferred_element_type=F32)
            for i in range(2):
                dst[:, :, b + i] = v[:, i * BLOCK:(i + 1) * BLOCK].reshape(NZ, NX, 8, BLOCK)

    order = far_first(NZ) + [0]
    load_rrhs.wait()
    rhs_t[...] = rrhs_v[...].astype(F32).T.astype(BF)
    load_theirs.wait()
    partial(1 - k, cs)
    load_ours.wait()
    partial(k, own)
    for cp in loads[3:]:
        cp.start()
    pl.semaphore_wait(barrier, len(peers))
    for d in order:
        send(cs.at[zd(d)], cr.at[zd(d)], csem, (d,), dev_c)

    for d in order:
        arrived(cr.at[zd(d)], csem, (d,))
        if d:
            ws[d] = (own[zd(d), :, AB:] + cr[zd(d), :, AB:]).astype(BF)
            send(ws.at[d], wr.at[d], wsem, (d,), dev_z(d), to=(0,))
        for e in far_first(NX):
            xs[d, e] = (own[zd(d), xd(e), :AB] + cr[zd(d), xd(e), :AB]).astype(BF)
            send(xs.at[d, e], xr.at[d, e], xsem, (d, e), dev_x(e), to=(d, 0))
    for d in order:
        acc = own[zd(d), x, :AB] + cr[zd(d), x, :AB]
        arrived(xr.at[d, pl.ds(1, NX - 1)], xsem, (d, 0))
        for e in range(1, NX):
            acc = acc + xr[d, e].astype(F32)
        if d:
            zs[d] = acc.astype(BF)
            send(zs.at[d], zr.at[d], zsem, (d,), dev_z(d))
        else:
            own[z, x, :AB] = acc
    acc = own[z, :, AB:] + cr[z, :, AB:]
    arrived(wr.at[pl.ds(1, NZ - 1)], wsem, (0,))
    for d in range(1, NZ):
        acc = acc + wr[d].astype(F32)
    own[z, :, AB:] = acc
    for e in far_first(NX):
        ts[e] = own[z, xd(e), AB:].astype(BF)
        send(ts.at[e], tr.at[e], tsem, (e,), dev_x(e), to=(0,))

    def choose(t, _):
        cnt = jnp.int32(0)
        got = [jnp.int32(0)] * CAP
        for s in range(G):
            b = bmap_s[k, t * G + s] - r * NB
            inside = jnp.logical_and(b >= 0, b < NB)
            for j in range(CAP):
                got[j] = jnp.where(jnp.logical_and(inside, cnt == j), b, got[j])
            cnt = cnt + jnp.where(inside, 1, 0)
        for j in range(CAP):
            sel[t * CAP + j] = got[j]
        return 0

    load_map.wait()
    load_count.wait()
    lax.fori_loop(0, NY, choose, 0)

    acc = own[z, x, :AB]
    for d in far_first(NZ):
        arrived(zr.at[d], zsem, (d,))
        acc = acc + zr[d].astype(F32)
    sol[pl.ds(k * HB, AB)] = acc.astype(BF)
    acc = own[z, x, AB:]
    arrived(tr.at[pl.ds(1, NX - 1)], tsem, (0,))
    for e in range(1, NX):
        acc = acc + tr[e].astype(F32)
    sol[pl.ds(k * HB + AB, HB - AB)] = acc.astype(BF)
    mine = pl.ds(k * HB, HB)
    send(sol.at[mine], sol.at[mine], c2sem, (0,), dev_c)
    arrived(sol.at[pl.ds((1 - k) * HB, HB)], c2sem, (0,))

    for d in far_first(NY) + [0]:
        t = yd(d)
        for j in range(CAP):
            v = sol[sel[t * CAP + j]]
            if d:
                ysd[d, j] = v
            else:
                yrc[r * CAP + j] = v
        if d:
            send(ysd.at[d], yrc.at[pl.ds(r * CAP, CAP)], ysem, (d,), dev_y(d))

    ranges = [lax.div(bmap_s[k, r * G + s], jnp.int32(NB)) for s in range(G)]
    for s in range(G):
        rank = jnp.int32(0)
        for e in range(s):
            rank = rank + jnp.where(ranges[e] == ranges[s], 1, 0)
        pos[s] = ranges[s] * CAP + jnp.minimum(rank, CAP - 1)
    drain()
    for d in range(1, NY):
        arrived(yrc.at[pl.ds(yd(-d) * CAP, CAP)], ysem, (d,))
    for s in [*range(HA, G), *range(HA)]:
        v = yrc[pos[s]]
        alive = r * G + s < bcnt_s[k]
        v = jnp.where(alive, v.astype(F32), 0.0).astype(BF)
        if s < HA:
            ga[0, 0, s] = v
        else:
            gb[0, 0, s - HA] = v

    for e in far_first(NX):
        send(ga.at[0, 0], ga.at[0, e], agx, (e,), dev_x(e))
    for i in range(1, NZ):
        send(gb.at[0, 0], gb.at[0, i], agz, (i,), dev_z(near(i)))

    def spread(i):
        for e in range(1, NX):
            send(gb.at[0, i], gb.at[e, i], agc, (e, i), dev_x(e), to=(e, 0))

    spread(0)
    for e in range(1, NX):
        arrived(ga.at[0, e], agx, (e,))
    for i in range(1, NZ):
        send(ga.at[0], ga.at[i], aga, (i,), dev_z(near(i)))
    for i in range(1, NZ):
        arrived(gb.at[0, i], agz, (i,))
        spread(i)
    load_coup.wait()

    def place(lo, hi, i, e):
        q = zd(-near(i)) * NX + xd(-e)
        for s in range(lo, hi):
            lhs[q, :, s * BLOCK:(s + 1) * BLOCK] = ga[i, e, s] if s < HA else gb[e, i, s - HA]

    def product(lo, hi):
        cols = slice(lo * BLOCK, hi * BLOCK)
        return lax.dot_general(
            coup_v[:, cols], lhs[:, :, cols].reshape(sz.C, (hi - lo) * BLOCK), (((1,), (1,)), ((), ())),
            preferred_element_type=F32)

    for i in range(NZ):
        if i:
            arrived(ga.at[i], aga, (i,))
        for e in range(NX):
            place(0, HA, i, e)
        place(HA, G, i, 0)
    ycs[...] = product(0, HA).reshape(NY, sz.SY, sz.C)
    for e in range(1, NX):
        arrived(gb.at[e], agc, (e, 0))
        for i in range(NZ):
            place(HA, G, i, e)
    prod = product(HA, G)
    ycs[...] = ycs[...] + prod.reshape(NY, sz.SY, sz.C)
    for d in far_first(NY):
        y1s[d] = ycs[yd(d)].astype(BF)
        send(y1s.at[d], ycr.at[d], y1sem, (d,), dev_y(d))

    def first_block(zz):
        return (sz.TZ * zz) // BLOCK

    for d in far_first(NZ):
        send(sol.at[pl.ds(first_block(zd(d)), sz.SPAN)], o1.at[z], o1sem, (d,), dev_z(d))
    o1[z] = sol[pl.ds(first_block(z), sz.SPAN)]

    load_crhs.wait()
    crhs_f[...] = crhs_v[...].astype(F32).reshape(NY, sz.SY, sz.C)
    load_cinv.wait()
    for j in range(sz.T3 // BLOCK):
        cols = slice(j * BLOCK, (j + 1) * BLOCK)
        cit[cols, :] = cinv_v[:, cols].astype(F32).T.astype(BF)

    acc = ycs[r]
    for d in far_first(NY)[::-1]:
        arrived(ycr.at[d], y1sem, (d,))
        acc = acc + ycr[d].astype(F32)
    red[r] = (crhs_f[r] - acc).astype(BF)
    for d in far_first(NY):
        send(red.at[r], red.at[r], y2sem, (d,), dev_y(d))

    for d in range(1, NZ):
        arrived(o1.at[zd(-d)], o1sem, (d,))
    for d in range(1, NX):
        send(o1, o2.at[x], o2sem, (d,), dev_x(d))
    o2[x] = o1[...]
    drain()
    for d in range(1, NX):
        arrived(o2.at[xd(-d)], o2sem, (d,))
    for b in range(sz.SPAN):
        v = jnp.stack([o2[e, :, b] for e in range(NX)], axis=1)
        ot[b * BLOCK:(b + 1) * BLOCK, :] = v.astype(F32).reshape(sz.C, BLOCK).T
    first_row = sz.TZ * z + (2 * x + k) * sz.TO - first_block(z) * BLOCK
    out[:sz.TO] = ot[pl.ds(pl.multiple_of(first_row, 8), sz.TO), :].astype(BF)

    for d in range(1, NY):
        arrived(red.at[yd(-d)], y2sem, (d,))
    reduced = red[...].astype(F32).reshape(sz.S3, sz.C).astype(BF)
    rows_z = NX * sz.TC
    for d in order:
        rows = pl.ds(pl.multiple_of(zd(d) * rows_z, rows_z), rows_z)
        v = jnp.dot(cit[rows, :], reduced, preferred_element_type=F32)
        p5f[d] = v.reshape(NX, sz.TC, sz.C)
        if d:
            w5s[d] = p5f[d, :, RA:].astype(BF)
            send(w5s.at[d], w5r.at[d], w5sem, (d,), dev_z(d), to=(0,))
        for e in far_first(NX):
            p5s[d, e] = p5f[d, xd(e), :RA].astype(BF)
            send(p5s.at[d, e], p5r.at[d, e], p5sem, (d, e), dev_x(e), to=(d, 0))
    for d in order:
        acc = p5f[d, x, :RA]
        arrived(p5r.at[d, pl.ds(1, NX - 1)], p5sem, (d, 0))
        for e in range(1, NX):
            acc = acc + p5r[d, e].astype(F32)
        if d:
            z5s[d] = acc.astype(BF)
            send(z5s.at[d], z5r.at[d], z5sem, (d,), dev_z(d))
    p5f[0, x, :RA] = acc
    acc = p5f[0, :, RA:]
    arrived(w5r.at[pl.ds(1, NZ - 1)], w5sem, (0,))
    for d in range(1, NZ):
        acc = acc + w5r[d].astype(F32)
    p5f[0, :, RA:] = acc
    for e in far_first(NX):
        t5s[e] = p5f[0, xd(e), RA:].astype(BF)
        send(t5s.at[e], t5r.at[e], t5sem, (e,), dev_x(e), to=(0,))
    drain()
    acc = p5f[0, x, :RA]
    for d in far_first(NZ):
        arrived(z5r.at[d], z5sem, (d,))
        acc = acc + z5r[d].astype(F32)
    out[sz.TO:sz.TO + RA] = acc.astype(BF)
    acc = p5f[0, x, RA:]
    arrived(t5r.at[pl.ds(1, NX - 1)], t5sem, (0,))
    for e in range(1, NX):
        acc = acc + t5r[e].astype(F32)
    out[sz.TO + RA:] = acc.astype(BF)


def per_device(mesh, root_rhs, root_inverse, child_rhs, child_inverse, coupling, block_map, block_count):
    sz = Sizes(mesh, root_rhs, root_inverse, child_inverse, coupling)
    coupling = jnp.swapaxes(coupling, 1, 2)
    NX, NZ, NY, HB, Q, G, HA = sz.NX, sz.NZ, sz.NY, sz.HB, sz.Q, sz.G, sz.HA
    AB, RA = sz.AB, sz.RA
    vmem = pl.BlockSpec(memory_space=pltpu.VMEM)
    hbm = pl.BlockSpec(memory_space=pl.ANY)

    def dma(*shape):
        return pltpu.SemaphoreType.DMA((2,) + shape)

    scratch = dict(
        rrhs_v=pltpu.VMEM((sz.S1, sz.C), BF),
        rinv_v=pltpu.VMEM((sz.S1, sz.T1), BF),
        crhs_v=pltpu.VMEM((sz.S3, sz.C), BF),
        coup_v=pltpu.VMEM((sz.S3, sz.U), BF),
        cinv_v=pltpu.VMEM((sz.S3, sz.T3), BF),
        bmap_s=pltpu.SMEM(block_map.shape, jnp.int32),
        bcnt_s=pltpu.SMEM(block_count.shape, jnp.int32),
        cit=pltpu.VMEM((sz.T3, sz.S3), BF),
        rhs_t=pltpu.VMEM((sz.C, sz.S1), BF),
        crhs_f=pltpu.VMEM((NY, sz.SY, sz.C), F32),
        cs=pltpu.VMEM((NZ, NX, HB, 8, BLOCK), F32),
        cr=pltpu.VMEM((NZ, NX, HB, 8, BLOCK), F32),
        own=pltpu.VMEM((NZ, NX, HB, 8, BLOCK), F32),
        xs=pltpu.VMEM((NZ, NX, AB, 8, BLOCK), BF),
        xr=pltpu.VMEM((NZ, NX, AB, 8, BLOCK), BF),
        zs=pltpu.VMEM((NZ, AB, 8, BLOCK), BF),
        zr=pltpu.VMEM((NZ, AB, 8, BLOCK), BF),
        ws=pltpu.VMEM((NZ, NX, HB - AB, 8, BLOCK), BF),
        wr=pltpu.VMEM((NZ, NX, HB - AB, 8, BLOCK), BF),
        ts=pltpu.VMEM((NX, HB - AB, 8, BLOCK), BF),
        tr=pltpu.VMEM((NX, HB - AB, 8, BLOCK), BF),
        sol=pltpu.VMEM((sz.NB, 8, BLOCK), BF),
        ysd=pltpu.VMEM((NY, CAP, 8, BLOCK), BF),
        yrc=pltpu.VMEM((NY * CAP, 8, BLOCK), BF),
        ga=pltpu.VMEM((NZ, NX, HA, 8, BLOCK), BF),
        gb=pltpu.VMEM((NX, NZ, G - HA, 8, BLOCK), BF),
        lhs=pltpu.VMEM((Q, 8, sz.U), BF),
        ycs=pltpu.VMEM((NY, sz.SY, sz.C), F32),
        y1s=pltpu.VMEM((NY, sz.SY, sz.C), BF),
        ycr=pltpu.VMEM((NY, sz.SY, sz.C), BF),
        red=pltpu.VMEM((NY, sz.SY, sz.C), BF),
        o1=pltpu.VMEM((NZ, sz.SPAN, 8, BLOCK), BF),
        o2=pltpu.VMEM((NX, NZ, sz.SPAN, 8, BLOCK), BF),
        ot=pltpu.VMEM((sz.SPAN * BLOCK, sz.C), F32),
        p5f=pltpu.VMEM((NZ, NX, sz.TC, sz.C), F32),
        p5s=pltpu.VMEM((NZ, NX, RA, sz.C), BF),
        p5r=pltpu.VMEM((NZ, NX, RA, sz.C), BF),
        z5s=pltpu.VMEM((NZ, RA, sz.C), BF),
        z5r=pltpu.VMEM((NZ, RA, sz.C), BF),
        w5s=pltpu.VMEM((NZ, NX, sz.TC - RA, sz.C), BF),
        w5r=pltpu.VMEM((NZ, NX, sz.TC - RA, sz.C), BF),
        t5s=pltpu.VMEM((NX, sz.TC - RA, sz.C), BF),
        t5r=pltpu.VMEM((NX, sz.TC - RA, sz.C), BF),
        sel=pltpu.SMEM((NY * CAP,), jnp.int32),
        pos=pltpu.SMEM((G,), jnp.int32),
        lsem=pltpu.SemaphoreType.DMA((8,)),
        csem=dma(NZ),
        xsem=dma(NZ, NX),
        zsem=dma(NZ),
        wsem=dma(NZ),
        tsem=dma(NX),
        c2sem=dma(1),
        ysem=dma(NY),
        o1sem=dma(NZ),
        o2sem=dma(NX),
        agx=dma(NX),
        aga=dma(NZ),
        agz=dma(NZ),
        agc=dma(NX, NZ),
        y1sem=dma(NY),
        y2sem=dma(NY),
        p5sem=dma(NZ, NX),
        z5sem=dma(NZ),
        w5sem=dma(NZ),
        t5sem=dma(NX),
    )
    names = list(scratch)

    def body(*refs):
        kernel(sz, *refs[:8], **dict(zip(names, refs[8:])))

    both = pl.pallas_call(
        body,
        name="backward",
        out_shape=pltpu.VMEM((sz.TO + sz.TC, sz.C), BF),
        in_specs=[hbm] * 7,
        out_specs=vmem,
        scratch_shapes=list(scratch.values()),
        compiler_params=pltpu.CompilerParams(
            collective_id=0, has_side_effects=True, vmem_limit_bytes=56 * 1024 * 1024
        ),
    )(root_rhs, root_inverse, child_rhs, child_inverse, coupling, block_map, block_count)
    return both[:sz.TO], both[sz.TO:][None]


def solution(mesh):
    in_specs = (
        P(("col", "cores"), None),
        P(("col", "cores"), "row"),
        P("cores", "col", None),
        P("cores", "col", "row"),
        P("cores", "row", "col"),
        P(),
        P(),
    )
    out_specs = (P(("row", "col", "cores"), None), P("cores", ("row", "col"), None))
    return jax.shard_map(
        functools.partial(per_device, mesh),
        mesh=mesh, in_specs=in_specs, out_specs=out_specs, check_vma=False,
    )
```
